32 devices in a mesh: dp: 8 (over z, y), pair: 4 (over x, core).
Axes of the slice: x: 2, y: 2, z: 4, core: 2. Of those that a mesh axis runs over, the one named last changes fastest.
Arguments:
- student_image: bfloat16 [8192, 512], P(('dp', 'pair')), may hold values from -60 to 60
- student_text: bfloat16 [8192, 512], P(('dp', 'pair')), may hold values from -6 to 6
- teacher_image: bfloat16 [8192, 1280], P(('dp', 'pair')), may hold values from -60 to 60
- teacher_text: bfloat16 [8192, 1280], P(('dp', 'pair')), may hold values from -6 to 6
Outputs:
- grad_image: float32 [8192, 512], P(('dp', 'pair'))
- grad_text: float32 [8192, 512], P(('dp', 'pair'))
The draws below stay inside these ranges and needn't reach their ends.
All inputs are finite; a program needn't handle non-finite values.
Results may differ from the reference program's by a relative error of at most 0.0025.
Values may be sent and summed in bfloat16 or wider, within the bound.
No kernel may reach another device: no remote copies, remote signals or barrier semaphores. Data moves between devices by JAX's collectives and lax.ppermute only.
A program may use at most 128 MiB of HBM per device.

```python
import math
import jax
import jax.numpy as jnp
from jax import lax

DS = 512
DT = 1280
WINDOW = 4
BLK = 1024
BATCH = 8192


def text_draw(key, salt, width):
    inner = jax.random.fold_in(key, salt)
    return jnp.clip(jax.random.normal(inner, (BATCH, width), jnp.float32), -6.0, 6.0)


def image_draw(key, salt, width):
    inner = jax.random.fold_in(key, salt)
    values = jax.random.normal(inner, (BATCH, width), jnp.float32)
    return jnp.clip(values, -60.0, 60.0)


def draw_student_text(key, part):
    return text_draw(key, 11, DS).astype(jnp.bfloat16)


def draw_teacher_text(key, part):
    return text_draw(key, 12, DT).astype(jnp.bfloat16)


def draw_student_image(key, part):
    return image_draw(key, 13, DS).astype(jnp.bfloat16)


def draw_teacher_image(key, part):
    return image_draw(key, 14, DT).astype(jnp.bfloat16)


def setup_inputs(seed: int = 0) -> dict:
    streams_of = jax.random.split(jax.random.key(seed), 5)
    return {
        "student_image": draw_student_image(jax.random.fold_in(streams_of[4], 71), 0),
        "student_text": draw_student_text(jax.random.fold_in(streams_of[4], 71), 0),
        "teacher_image": draw_teacher_image(jax.random.fold_in(streams_of[4], 71), 0),
        "teacher_text": draw_teacher_text(jax.random.fold_in(streams_of[4], 71), 0),
    }


def stats_of(scores, axis):
    top = lax.optimization_barrier(jnp.max(scores, axis=axis))
    total = lax.optimization_barrier(jnp.sum(jnp.exp(scores - jnp.expand_dims(top, axis)), axis=axis))
    return (top, total)

def combine_stats(first, second):
    result = []
    for offset in (0, 2):
        top = jnp.maximum(first[offset], second[offset])
        total = first[offset + 1] * jnp.exp(first[offset] - top) + second[offset + 1] * jnp.exp(second[offset] - top)
        result += [top, total]
    return tuple(result)

def reference(student_image, student_text, teacher_image, teacher_text):
    scale_s = 2.0 / math.sqrt(DS)
    scale_t = 2.0 / math.sqrt(DT)
    blocks = BATCH // BLK
    span = WINDOW * BLK
    starts = jnp.arange(blocks, dtype=jnp.int32) * BLK
    text_s = jnp.concatenate([student_text, student_text[:span]], axis=0)
    text_t = jnp.concatenate([teacher_text, teacher_text[:span]], axis=0)

    def tiles(first):
        rows_s = lax.dynamic_slice_in_dim(student_image, first, BLK, 0)
        rows_t = lax.dynamic_slice_in_dim(teacher_image, first, BLK, 0)
        win_s = lax.dynamic_slice_in_dim(text_s, first, span, 0)
        win_t = lax.dynamic_slice_in_dim(text_t, first, span, 0)
        s_tile = jnp.dot(rows_s, win_s.T, preferred_element_type=jnp.float32) * scale_s
        t_tile = jnp.dot(rows_t, win_t.T, preferred_element_type=jnp.float32) * scale_t
        return (rows_s, win_s, s_tile, t_tile)

    def first_pass(carry, first):
        rows_s, win_s, s_tile, t_tile = tiles(first)
        row_stats = stats_of(s_tile, 1) + stats_of(t_tile, 1)
        old = tuple((lax.dynamic_slice_in_dim(c, first, span, 0) for c in carry))
        new = combine_stats(old, stats_of(s_tile, 0) + stats_of(t_tile, 0))
        carry = tuple((lax.dynamic_update_slice_in_dim(c, n, first, 0) for c, n in zip(carry, new)))
        return (carry, row_stats)
    low = jnp.full((BATCH + span,), -1e+30, jnp.float32)
    nothing = jnp.zeros((BATCH + span,), jnp.float32)
    columns, rows = lax.scan(first_pass, (low, nothing, low, nothing), starts)
    head = tuple((c[:span] for c in columns))
    tail = tuple((c[BATCH:] for c in columns))
    folded = combine_stats(head, tail)
    whole = tuple((jnp.concatenate([f, c[span:BATCH]], axis=0) for f, c in zip(folded, columns)))
    extended = tuple((jnp.concatenate([c, c[:span]], axis=0) for c in whole))

    def second_pass(text_acc, packed):
        first, rm_s, rz_s, rm_t, rz_t = packed
        rows_s, win_s, s_tile, t_tile = tiles(first)
        cm_s, cz_s, cm_t, cz_t = tuple((lax.dynamic_slice_in_dim(c, first, span, 0) for c in extended))
        weights = (jnp.exp(s_tile - rm_s[:, None]) / rz_s[:, None] - jnp.exp(t_tile - rm_t[:, None]) / rz_t[:, None] + jnp.exp(s_tile - cm_s[None, :]) / cz_s[None, :] - jnp.exp(t_tile - cm_t[None, :]) / cz_t[None, :]).astype(jnp.bfloat16)
        image_part = jnp.dot(weights, win_s, preferred_element_type=jnp.float32)
        old = lax.dynamic_slice_in_dim(text_acc, first, span, 0)
        added = old + jnp.dot(weights.T, rows_s, preferred_element_type=jnp.float32)
        text_acc = lax.dynamic_update_slice_in_dim(text_acc, added, first, 0)
        return (text_acc, image_part)
    text_acc, image_parts = lax.scan(second_pass, jnp.zeros((BATCH + span, DS), jnp.float32), (starts,) + rows)
    text_sum = text_acc[:BATCH].at[:span].add(text_acc[BATCH:])
    grad_image = image_parts.reshape(BATCH, DS) * scale_s
    grad_text = text_sum * scale_s
    return (grad_image, grad_text)
```

```python
import math

import jax
import jax.numpy as jnp
from jax import lax
from jax.experimental import pallas as pl
from jax.experimental.pallas import tpu as pltpu
from jax.sharding import PartitionSpec as P

AXES = ("dp", "pair")
MIB = 1024 * 1024
LOG2E = math.log2(math.e)
HEAVY = pl.CostEstimate(flops=10**11, bytes_accessed=10**9, transcendentals=0)
LIGHT = pl.CostEstimate(flops=3 * 10**9, bytes_accessed=3 * 10**7, transcendentals=0)


def send_to(value, place):
    count = lax.axis_size("dp")
    pairs = []
    for block in range(count):
        for member in range(4):
            to_block, to_x, to_core = place(block, member // 2, member % 2)
            pairs.append((block * 4 + member, (to_block % count) * 4 + to_x * 2 + to_core))
    return lax.ppermute(value, AXES, pairs)


def to_other_core(value):
    return send_to(value, lambda block, x, core: (block, x, 1 - core))


def to_other_x(value):
    return send_to(value, lambda block, x, core: (block, 1 - x, core))


def ahead(value, steps):
    return send_to(value, lambda block, x, core: (block + steps, x, core))


def joined(first, second):
    rows = []
    for offset in (0, 2):
        rows += merged(first[offset : offset + 2], second[offset : offset + 2])
    return rows


def pack_kernel(first, second, whole, *halves):
    width = first.shape[1]
    half = first.shape[0] // 2
    whole[:, :width] = first[...]
    whole[:, width:] = second[...]
    for index, out in enumerate(halves):
        here = pl.ds(index * half, half)
        out[:, :width] = first[here]
        out[:, width:] = second[here]


def pack_arrived_kernel(s_ahead, t_ahead, s_x, t_x, ahead_out, rest_out, x_out, part_out):
    width, first = s_x.shape[1], part_out.shape[0]
    for student, teacher, whole, part, here in (
        (s_ahead, t_ahead, ahead_out, rest_out, pl.ds(first, s_x.shape[0] - first)),
        (s_x, t_x, x_out, part_out, pl.ds(0, first)),
    ):
        whole[:, :width] = student[...]
        whole[:, width:] = teacher[...]
        part[:, :width] = student[here]
        part[:, width:] = teacher[here]


def rows_of(parts, columns):
    parts = [part[:, columns] for part in parts]
    return parts[0] if len(parts) == 1 else jnp.concatenate(parts, axis=0)


def tile_of(image, texts, span, scale):
    parts = [
        lax.dot_general(
            image,
            rows_of(text, span),
            (((1,), (1,)), ((), ())),
            preferred_element_type=jnp.float32,
        )
        for text in texts
    ]
    tile = parts[0] if len(parts) == 1 else jnp.concatenate(parts, axis=1)
    return tile * (scale * LOG2E)


def stats_along(tile, axis):
    top = jnp.max(tile, axis=axis, keepdims=True)
    below = jnp.exp2(tile - top)
    return top, jnp.sum(below, axis=axis, keepdims=True), below


def merged(first, second):
    top = jnp.maximum(first[0], second[0])
    return top, first[1] * jnp.exp2(first[0] - top) + second[1] * jnp.exp2(second[0] - top)


def as_rows(columns, shard):
    lane = lax.broadcasted_iota(jnp.int32, (shard, 128), 1)
    packed = jnp.zeros((shard, 128), jnp.float32)
    for k, column in enumerate(columns):
        packed = jnp.where(lane == k, column, packed)
    return packed.T[:8]


def score_shards(images, texts, spans, scales, outs, shard):
    stats = [([], []) for _ in images]
    waiting = None
    for step in [(index, which) for index in range(len(images)) for which in range(2)] + [None]:
        tile = None
        if step:
            index, which = step
            image = rows_of(images[index], spans[which])
            tile = tile_of(image, texts, spans[which], scales[which])
        if waiting:
            (index, which), old = waiting
            here = pl.ds(index * shard, shard)
            for axis, found in ((1, stats[index][0]), (0, stats[index][1])):
                top, total, outs[2 * which + 1 - axis][here] = stats_along(old, axis)
                found += (top, total)
        waiting = step, tile
    return stats


def rows4(ref, first, columns=slice(None)):
    part = ref[first : first + 4, columns]
    return [part[k : k + 1] for k in range(4)]


def text_parts(refs, count):
    whole = count - 1
    texts = [(ref,) for ref in refs[:whole]]
    if count == 3:
        return texts + [refs[whole : whole + 1]], refs[whole + 1 :]
    return texts + [refs[whole : whole + 2]], refs[whole + 2 :]


def part_kernel(shard, scales, spans, size, count, *refs):
    images, refs = (refs[:size], refs[size : 2 * size]), refs[2 * size :]
    texts, refs = text_parts(refs, count)
    others, refs = (refs[:4], refs[4:]) if len(refs) > 6 else ((), refs)
    outs, (row_out, col_out), stat_out = refs[:4], refs[4:6], refs[6:]
    stats = score_shards(images, texts, spans, scales, outs, shard)
    for index, (row, column) in enumerate(stats):
        row_out[:, pl.ds(index * shard, shard)] = as_rows(row, shard)
        for k, value in enumerate(column):
            col_out[4 * index + k : 4 * index + k + 1] = value
    if not others:
        return
    row_home, col_home, row_side, col_side = others
    rows = joined(rows4(row_home, 0), rows4(row_side, 0))
    columns = joined(rows4(col_out, 0), rows4(col_out, 4))
    seen = joined(rows4(col_home, 0), rows4(col_home, 4))
    seen = joined(seen, [part[:, : 3 * shard] for part in columns])
    last = joined(rows4(col_side, 0), rows4(col_side, 4))
    last = joined(last, [part[:, 3 * shard :] for part in columns])
    for k in range(4):
        stat_out[0][k : k + 1, : 2 * shard] = rows[k]
        stat_out[0][k : k + 1, 2 * shard :] = row_out[k : k + 1]
        stat_out[0][4 + k : 5 + k, : 3 * shard] = seen[k]
        stat_out[0][4 + k : 5 + k, 3 * shard :] = last[k]


def piece_stats(ref, kind, piece, shard):
    part = ref[4 * kind : 4 * kind + 4, piece * shard : (piece + 1) * shard]
    return [part[k : k + 1] for k in range(4)]


def block_parities():
    block = lax.axis_index("dp")
    return lax.rem(block, 2) == 0, lax.rem(block // 2, 2) == 0


def join_group_kernel(shard, mine_ref, core_ref, x_ref, home_ref, *outs):
    halves = []
    for kind, other_ref in enumerate((core_ref, x_ref)):
        for half in range(2):
            joint = []
            for piece in (2 * half, 2 * half + 1):
                total = joined(
                    piece_stats(mine_ref, kind, piece, shard),
                    piece_stats(other_ref, kind, piece ^ 1, shard),
                )
                for k, value in enumerate(total):
                    at = 4 * kind + k
                    home_ref[at : at + 1, piece * shard : (piece + 1) * shard] = value
                joint.append(total)
            halves.append([jnp.concatenate(pair, axis=1) for pair in zip(*joint)])
    for kind, upward in enumerate(block_parities()):
        up, down = halves[2 * kind + kind], halves[2 * kind + 1 - kind]
        for k in range(4):
            outs[2 * kind][k : k + 1] = jnp.where(upward, up[k], down[k])
            outs[2 * kind + 1][k : k + 1] = jnp.where(upward, down[k], up[k])
        for out in outs[2 * kind : 2 * kind + 2]:
            out[4:8] = jnp.zeros((4, 2 * shard), jnp.float32)


def join_blocks_kernel(shard, home_ref, *refs):
    ins, out = refs[:4], refs[4]
    for kind, upward in enumerate(block_parities()):
        first, second = (rows4(ref, 0) for ref in ins[2 * kind : 2 * kind + 2])
        above = [jnp.where(upward, x, y) for x, y in zip(first, second)]
        below = [jnp.where(upward, y, x) for x, y in zip(first, second)]
        for half in range(2):
            here = slice(2 * half * shard, 2 * (half + 1) * shard)
            total = joined(rows4(home_ref, 4 * kind, here), above if half == kind else below)
            for k, value in enumerate(total):
                at = 4 * kind + k
                out[at : at + 1, here] = value


def row_factors(stat_ref, tops, index, shard):
    max_s, total_s, max_t, total_t = rows4(stat_ref, 0, pl.ds(index * shard, shard))
    sub = lax.broadcasted_iota(jnp.int32, (128, shard), 0)
    packed = jnp.zeros((128, shard), jnp.float32)
    for k, (top_s, _, top_t, _) in enumerate(tops):
        packed = jnp.where(sub == 2 * k, jnp.exp2(top_s - max_s) / total_s, packed)
        packed = jnp.where(sub == 2 * k + 1, jnp.exp2(top_t - max_t) / total_t, packed)
    packed = packed.T
    return [packed[:, k : k + 1] for k in range(2 * len(tops))]


def weigh(below, here, columns, row, tops, stats):
    row_s, col_s, row_t, col_t = (ref[here, columns] for ref in below)
    top_s, _, top_t, _ = tops
    max_s, total_s, max_t, total_t = stats
    return (
        row_s * row[0]
        - row_t * row[1]
        + col_s * (jnp.exp2(top_s - max_s) / total_s)
        - col_t * (jnp.exp2(top_t - max_t) / total_t)
    ).astype(jnp.bfloat16)


def text_term(image, weights):
    return lax.dot_general(
        image, weights, (((0,), (0,)), ((), ())), preferred_element_type=jnp.float32
    )


def image_term(weights, texts, span):
    total = None
    for index, text in enumerate(texts):
        shard = weights[0].shape[1] // 2
        part = jnp.dot(
            weights[index // 2][:, (index % 2) * shard : (index % 2 + 1) * shard],
            rows_of(text, span),
            preferred_element_type=jnp.float32,
        )
        total = part if total is None else total + part
    return total


def ahead_kernel(shard, span, *refs):
    below_home, below_side, below_behind = refs[0:4], refs[4:8], refs[8:12]
    rows_in, cols_in, stat_ref = refs[12:18:2], refs[13:18:2], refs[18]
    images = (refs[19:20], refs[20:21], refs[21:23], refs[23:25])
    texts, refs = text_parts(refs[25:], 4)
    same_out, cross_out, weights_out, img_out, both_out = (
        refs[0:2], refs[2:4], refs[4], refs[5:7], refs[7]
    )
    home, third = slice(0, 2 * shard), slice(2 * shard, 3 * shard)
    fourth, far = slice(3 * shard, 4 * shard), slice(2 * shard, 4 * shard)
    col_home, col_third, col_last, col_far = (
        rows4(stat_ref, 4, at) for at in (home, third, fourth, far)
    )

    def weights_of(index):
        here = pl.ds((index % 2) * shard, shard)
        at = 4 * (index % 2)
        if index < 2:
            tops = (rows4(rows_in[0], 0, here), rows4(rows_in[1], 0, here))
            row = row_factors(stat_ref, tops, index, shard)
            seen = rows4(cols_in[0], at, third)
            weights = jnp.concatenate(
                [
                    weigh(below_home, here, third, row[:2], seen, col_third),
                    weigh(
                        below_side, here, slice(None), row[2:], rows4(cols_in[1], at), col_last
                    ),
                ],
                axis=1,
            )
        else:
            row = row_factors(stat_ref, (rows4(rows_in[2], 0, here),), index, shard)
            weights = weigh(below_behind, here, far, row, rows4(cols_in[2], at, far), col_far)
            near = weigh(below_behind, here, home, row, rows4(cols_in[2], at, home), col_home)
        return weights, None if index < 2 else near

    total = both = None
    ready = weights_of(0)
    for index in range(4):
        weights, near = ready
        if index < 3:
            ready = weights_of(index + 1)
        image = rows_of(images[index], span)
        term = text_term(image, weights)
        total = total + term if index else term
        if index < 2:
            weights_out[pl.ds(index * shard, shard)] = weights
            continue
        term = text_term(image, near)
        both = term if index == 2 else both + term
        out = img_out[index - 2]
        out[...] = image_term((near, weights), texts, span).astype(out.dtype)
    height = total.shape[0] // 2
    for index in range(2):
        part = total[index * height : (index + 1) * height]
        same_out[index][...] = part[:, :shard]
        cross_out[index][...] = part[:, shard:].astype(jnp.bfloat16)
    both_out[...] = both


def home_kernel(shard, span, *refs):
    below, (row_in, col_in, stat_ref) = refs[0:4], refs[4:7]
    images = (refs[7:8], refs[8:9])
    texts, (weights_in, both_in, *outs) = text_parts(refs[9:], 4)
    img_out, txt_own, txt_x = outs[0:2], *outs[2:]
    home = slice(0, 2 * shard)
    col_home = rows4(stat_ref, 4, home)
    total = both_in[...]
    for index in range(2):
        here = pl.ds(index * shard, shard)
        row = row_factors(stat_ref, (rows4(row_in, 0, here),), index, shard)
        tops = rows4(col_in, 4 * index, home)
        weights = weigh(below, here, home, row, tops, col_home)
        total = total + text_term(rows_of(images[index], span), weights)
        out = img_out[index]
        out[...] = image_term((weights, weights_in[here]), texts, span).astype(out.dtype)
    txt_own[...] = total[:, :shard]
    txt_x[...] = total[:, shard:].astype(jnp.bfloat16)


def add_kernel(first, second, out):
    total = first[...] + second[...].astype(jnp.float32)
    out[...] = total.astype(out.dtype)


def finish_image_kernel(scale, own, core, home, out):
    total = own[...] + core[...].astype(jnp.float32)
    out[...] = (total + home[...].astype(jnp.float32)) * scale


def finish_text_kernel(scale, own, *refs):
    homes, out = refs[:-1], refs[-1]
    width = homes[0].shape[0]
    for index, home in enumerate(homes):
        here = slice(index * width, (index + 1) * width)
        total = own[here] + home[...].astype(jnp.float32)
        out[:, here] = total.T * scale


def on_device(student_image, student_text, teacher_image, teacher_text):
    shard, width_s = student_image.shape
    width_t = teacher_image.shape[1]
    scale_s = 2.0 / math.sqrt(width_s)
    scale_t = 2.0 / math.sqrt(width_t)
    f32 = jnp.float32
    bf16 = jnp.bfloat16
    vmem = pl.BlockSpec(memory_space=pltpu.VMEM)

    def params(mib):
        return pltpu.CompilerParams(vmem_limit_bytes=mib * MIB)


    spans = (slice(0, width_s), slice(width_s, width_s + width_t))
    scales = (scale_s, scale_t)

    def pack(first, second, halves, name):
        heights = (shard,) + (shard // 2,) * halves
        return pl.pallas_call(
            pack_kernel,
            out_shape=tuple(
                jax.ShapeDtypeStruct((height, width_s + width_t), bf16) for height in heights
            ),
            in_specs=[vmem] * 2,
            out_specs=(vmem,) * len(heights),
            compiler_params=params(8),
            name=name,
        )(first, second)

    text_t_ahead, text_t_x = ahead(teacher_text, -2), to_other_x(teacher_text)
    text_s_ahead, text_s_x = ahead(student_text, -2), to_other_x(student_text)
    image_s_core, image_t_core = to_other_core(student_image), to_other_core(teacher_image)
    image, top, bottom = pack(student_image, teacher_image, 2, "pack_images")
    top, image_s_core, image_t_core = lax.optimization_barrier((top, image_s_core, image_t_core))
    top = send_to(top, lambda block, x, core: (block ^ 1, x, core))
    top, bottom, late_s, late_t = lax.optimization_barrier(
        (top, bottom, text_s_ahead, text_t_ahead, text_s_x, text_t_x)
    )[:4]
    packed, first = width_s + width_t, shard // 8
    text_ahead, rest, text_x, text_part = pl.pallas_call(
        pack_arrived_kernel,
        out_shape=tuple(
            jax.ShapeDtypeStruct((height, packed), bf16)
            for height in (shard, shard - first, shard, first)
        ),
        in_specs=[vmem] * 4,
        out_specs=(vmem,) * 4,
        compiler_params=params(8),
        name="pack_arrived",
    )(late_s, late_t, text_s_x, text_t_x)
    (text,) = pack(student_text, teacher_text, 0, "pack_own")
    (image_core,) = pack(image_s_core, image_t_core, 0, "pack_core")

    def stat(shards):
        return jax.ShapeDtypeStruct((8, shards * shard), f32)

    def score(rows, columns):
        return jax.ShapeDtypeStruct((rows * shard, columns * shard), f32)

    def part_scores(shards, texts, *others, name, cost=None):
        size, count = len(shards[0]), {3: 3, 2: 1, 5: 4}[len(texts)]
        outs = (score(2, count),) * 4 + (stat(2), stat(count)) + (stat(4),) * bool(others)
        return pl.pallas_call(
            lambda *refs: part_kernel(shard, scales, spans, size, count, *refs),
            out_shape=outs,
            in_specs=[vmem] * (2 * size + len(texts) + len(others)),
            out_specs=(vmem,) * len(outs),
            compiler_params=params(16),
            cost_estimate=cost,
            name=name,
        )(*shards[0], *shards[1], *texts, *others)

    text_both = (ahead(text_part, -2), to_other_x(rest))
    top = send_to(top, lambda block, x, core: (block + 2 - block % 2 * 2, x, core))
    bottom = ahead(bottom, 1)
    texts = (text, text_x, text_ahead, *text_both)
    own = ((image,), (image_core,))
    *below_home, row_home, col_home = part_scores(own, texts[:3], name="scores_home")
    *below_side, row_side, col_side = part_scores(own, texts[3:], name="scores_side", cost=HEAVY)
    top, bottom = lax.optimization_barrier((top, bottom, row_home))[:2]
    behind = ((top, bottom), (to_other_core(top), to_other_core(bottom)))
    images = (image, image_core, *behind[0], *behind[1])
    stats_own = (row_home, col_home, row_side, col_side)
    *below_behind, row_behind, col_behind, partial = part_scores(
        behind, texts, *stats_own, name="scores_behind"
    )

    shared = jax.ShapeDtypeStruct((8, 2 * shard), f32)
    home, *away = pl.pallas_call(
        lambda *refs: join_group_kernel(shard, *refs),
        out_shape=(stat(4),) + (shared,) * 4,
        in_specs=[vmem] * 3,
        out_specs=(vmem,) * 5,
        compiler_params=params(8),
        name="join_group",
    )(partial, to_other_core(partial), to_other_x(partial))
    away = [
        send_to(part, lambda block, x, core, step=step, first=first: (
            block + (step if (block // step) % 2 == first else -step), x, core
        ))
        for part, step, first in zip(away, (1, 1, 2, 2), (0, 1, 0, 1))
    ]
    stats = pl.pallas_call(
        lambda *refs: join_blocks_kernel(shard, *refs),
        out_shape=stat(4),
        in_specs=[vmem] * 5,
        out_specs=vmem,
        compiler_params=params(8),
        name="join_blocks",
    )(home, *away)

    wide = jax.ShapeDtypeStruct((shard, width_s), f32)
    tall = jax.ShapeDtypeStruct((width_s, shard), f32)
    sent = jax.ShapeDtypeStruct((width_s, shard), bf16)
    flat = jax.ShapeDtypeStruct((shard, width_s), bf16)
    tall_half = jax.ShapeDtypeStruct((width_s // 2, shard), f32)
    sent_half = jax.ShapeDtypeStruct((width_s // 2, shard), bf16)
    *txt_ahead, weights, img_back, img_cross, txt_both = pl.pallas_call(
        lambda *refs: ahead_kernel(shard, spans[0], *refs),
        out_shape=(
            tall_half,
            tall_half,
            sent_half,
            sent_half,
            jax.ShapeDtypeStruct((2 * shard, 2 * shard), bf16),
            wide,
            flat,
            jax.ShapeDtypeStruct((width_s, 2 * shard), f32),
        ),
        in_specs=[vmem] * 30,
        out_specs=(vmem,) * 8,
        compiler_params=params(24),
        name="gradients_ahead",
    )(
        *below_home, *below_side, *below_behind, *stats_own, row_behind, col_behind, stats,
        *images, *texts,
    )
    img_own, img_core, txt_own, txt_x = pl.pallas_call(
        lambda *refs: home_kernel(shard, spans[0], *refs),
        out_shape=(wide, flat, tall, sent),
        in_specs=[vmem] * 16,
        out_specs=(vmem,) * 4,
        compiler_params=params(24),
        name="gradients_home",
    )(*below_home, row_home, col_home, stats, *images[:2], *texts, weights, txt_both)

    img_cross = to_other_core(img_cross)
    img_sum = (img_back + img_cross.astype(f32)).astype(bf16)
    img_home = ahead(img_sum, -1)
    txt_same, txt_cross = txt_ahead[:2], [to_other_x(part) for part in txt_ahead[2:]]
    img_core = to_other_core(img_core)

    def add(first, second, out, name):
        return pl.pallas_call(
            add_kernel,
            out_shape=out,
            in_specs=[vmem] * 2,
            out_specs=vmem,
            compiler_params=params(8),
            cost_estimate=LIGHT,
            name=name,
        )(first, second)

    txt_cross[0] = lax.optimization_barrier((txt_cross[0], img_sum))[0]
    txt_sum = add(txt_same[0], txt_cross[0], sent_half, "add_text")
    txt_x, txt_cross[1] = lax.optimization_barrier((txt_x, txt_cross[1], txt_sum))[:2]
    txt_home = [
        ahead(txt_sum, 2), ahead(add(txt_same[1], txt_cross[1], sent_half, "add_text"), 2)
    ]
    txt_own = add(txt_own, to_other_x(txt_x), tall, "add_own_text")

    def finish(kernel, *args, name):
        return pl.pallas_call(
            lambda *refs: kernel(scale_s, *refs),
            out_shape=wide,
            in_specs=[vmem] * len(args),
            out_specs=vmem,
            compiler_params=params(8),
            name=name,
        )(*args)

    grad_image = finish(finish_image_kernel, img_own, img_core, img_home, name="finish_image")
    *txt_home, txt_own, grad_image = lax.optimization_barrier((*txt_home, txt_own, grad_image))
    grad_text = finish(finish_text_kernel, txt_own, *txt_home, name="finish_text")
    return (grad_image, grad_text)


def solution(mesh):
    spec = P(AXES, None)
    return jax.shard_map(
        on_device,
        mesh=mesh,
        in_specs=(spec, spec, spec, spec),
        out_specs=(spec, spec),
        check_vma=False,
    )
```

```python
import math

import jax
import jax.numpy as jnp
from jax import lax
from jax.experimental import pallas as pl
from jax.experimental.pallas import tpu as pltpu
from jax.sharding import PartitionSpec as P

AXES = ("dp", "pair")
MIB = 1024 * 1024
LOG2E = math.log2(math.e)
HEAVY = pl.CostEstimate(flops=10**11, bytes_accessed=10**9, transcendentals=0)
LIGHT = pl.CostEstimate(flops=3 * 10**9, bytes_accessed=3 * 10**7, transcendentals=0)


def send_to(value, place):
    count = lax.axis_size("dp")
    pairs = []
    for block in range(count):
        for member in range(4):
            to_block, to_x, to_core = place(block, member // 2, member % 2)
            pairs.append((block * 4 + member, (to_block % count) * 4 + to_x * 2 + to_core))
    return lax.ppermute(value, AXES, pairs)


def to_other_core(value):
    return send_to(value, lambda block, x, core: (block, x, 1 - core))


def to_other_x(value):
    return send_to(value, lambda block, x, core: (block, 1 - x, core))


def ahead(value, steps):
    return send_to(value, lambda block, x, core: (block + steps, x, core))


def joined(first, second):
    rows = []
    for offset in (0, 2):
        rows += merged(first[offset : offset + 2], second[offset : offset + 2])
    return rows


def pack_kernel(first, second, whole, *halves):
    width = first.shape[1]
    half = first.shape[0] // 2
    whole[:, :width] = first[...]
    whole[:, width:] = second[...]
    for index, out in enumerate(halves):
        here = pl.ds(index * half, half)
        out[:, :width] = first[here]
        out[:, width:] = second[here]


def pack_arrived_kernel(s_ahead, t_ahead, s_x, t_x, ahead_out, rest_out, x_out, part_out):
    width, first = s_x.shape[1], part_out.shape[0]
    for student, teacher, whole, part, here in (
        (s_ahead, t_ahead, ahead_out, rest_out, pl.ds(first, s_x.shape[0] - first)),
        (s_x, t_x, x_out, part_out, pl.ds(0, first)),
    ):
        whole[:, :width] = student[...]
        whole[:, width:] = teacher[...]
        part[:, :width] = student[here]
        part[:, width:] = teacher[here]


def rows_of(parts, columns):
    parts = [part[:, columns] for part in parts]
    return parts[0] if len(parts) == 1 else jnp.concatenate(parts, axis=0)


def tile_of(image, texts, span, scale):
    parts = [
        lax.dot_general(
            image,
            rows_of(text, span),
            (((1,), (1,)), ((), ())),
            preferred_element_type=jnp.float32,
        )
        for text in texts
    ]
    tile = parts[0] if len(parts) == 1 else jnp.concatenate(parts, axis=1)
    return tile * (scale * LOG2E)


def stats_along(tile, axis):
    top = jnp.max(tile, axis=axis, keepdims=True)
    below = jnp.exp2(tile - top)
    return top, jnp.sum(below, axis=axis, keepdims=True), below


def merged(first, second):
    top = jnp.maximum(first[0], second[0])
    return top, first[1] * jnp.exp2(first[0] - top) + second[1] * jnp.exp2(second[0] - top)


def as_rows(columns, shard):
    lane = lax.broadcasted_iota(jnp.int32, (shard, 128), 1)
    packed = jnp.zeros((shard, 128), jnp.float32)
    for k, column in enumerate(columns):
        packed = jnp.where(lane == k, column, packed)
    return packed.T[:8]


def score_shards(images, texts, spans, scales, outs, shard):
    stats = [([], []) for _ in images]
    waiting = None
    for step in [(index, which) for index in range(len(images)) for which in range(2)] + [None]:
        tile = None
        if step:
            index, which = step
            image = rows_of(images[index], spans[which])
            tile = tile_of(image, texts, spans[which], scales[which])
        if waiting:
            (index, which), old = waiting
            here = pl.ds(index * shard, shard)
            for axis, found in ((1, stats[index][0]), (0, stats[index][1])):
                top, total, outs[2 * which + 1 - axis][here] = stats_along(old, axis)
                found += (top, total)
        waiting = step, tile
    return stats


def rows4(ref, first, columns=slice(None)):
    part = ref[first : first + 4, columns]
    return [part[k : k + 1] for k in range(4)]


def text_parts(refs, count):
    whole = count - 1
    texts = [(ref,) for ref in refs[:whole]]
    if count == 3:
        return texts + [refs[whole : whole + 1]], refs[whole + 1 :]
    return texts + [refs[whole : whole + 2]], refs[whole + 2 :]


def part_kernel(shard, scales, spans, sizes, count, *refs):
    images = []
    for size in sizes:
        images.append(refs[:size])
        refs = refs[size:]
    texts, refs = text_parts(refs, count)
    outs, (row_out, col_out) = refs[:4], refs[4:]
    stats = score_shards(images, texts, spans, scales, outs, shard)
    for index, (row, column) in enumerate(stats):
        row_out[:, pl.ds(index * shard, shard)] = as_rows(row, shard)
        for k, value in enumerate(column):
            col_out[4 * index + k : 4 * index + k + 1] = value


def far_kernel(shard, scales, spans, *refs):
    outs = refs[13:]
    part_kernel(shard, scales, spans, (2,), 4, *refs[:7], *outs[:6])
    total_kernel(shard, *refs[7:13], outs[4], outs[5], outs[6])


HOME, NEAR, SIDE, FAR = range(4)


def join_calls(rows_in, cols_in, shard):
    rows = []
    for index in range(3):
        call, place = (HOME, index) if index < 2 else (NEAR, 0)
        first = rows4(rows_in[call], 0, pl.ds(place * shard, shard))
        rows.append(joined(first, rows4(rows_in[SIDE], 0, pl.ds(index * shard, shard))))
    rows.append(rows4(rows_in[FAR], 0))
    columns = rows4(cols_in[FAR], 0)
    seen = [part[:, : 3 * shard] for part in columns]
    last = [part[:, 3 * shard :] for part in columns]
    for call, place in ((HOME, 0), (HOME, 1), (NEAR, 0)):
        seen = joined(seen, rows4(cols_in[call], 4 * place))
    for place in range(3):
        last = joined(last, rows4(cols_in[SIDE], 4 * place))
    return rows, seen, last


def total_kernel(shard, *refs):
    rows, seen, last = join_calls(refs[0:8:2], refs[1:8:2], shard)
    out = refs[8]
    for k in range(4):
        for index in range(4):
            out[k : k + 1, index * shard : (index + 1) * shard] = rows[index][k]
        out[4 + k : 5 + k, : 3 * shard] = seen[k]
        out[4 + k : 5 + k, 3 * shard :] = last[k]


def piece_stats(ref, kind, piece, shard):
    part = ref[4 * kind : 4 * kind + 4, piece * shard : (piece + 1) * shard]
    return [part[k : k + 1] for k in range(4)]


def block_parities():
    block = lax.axis_index("dp")
    return lax.rem(block, 2) == 0, lax.rem(block // 2, 2) == 0


def join_group_kernel(shard, mine_ref, core_ref, x_ref, home_ref, *outs):
    halves = []
    for kind, other_ref in enumerate((core_ref, x_ref)):
        for half in range(2):
            joint = []
            for piece in (2 * half, 2 * half + 1):
                total = joined(
                    piece_stats(mine_ref, kind, piece, shard),
                    piece_stats(other_ref, kind, piece ^ 1, shard),
                )
                for k, value in enumerate(total):
                    at = 4 * kind + k
                    home_ref[at : at + 1, piece * shard : (piece + 1) * shard] = value
                joint.append(total)
            halves.append([jnp.concatenate(pair, axis=1) for pair in zip(*joint)])
    for kind, upward in enumerate(block_parities()):
        up, down = halves[2 * kind + kind], halves[2 * kind + 1 - kind]
        for k in range(4):
            outs[2 * kind][k : k + 1] = jnp.where(upward, up[k], down[k])
            outs[2 * kind + 1][k : k + 1] = jnp.where(upward, down[k], up[k])
        for out in outs[2 * kind : 2 * kind + 2]:
            out[4:8] = jnp.zeros((4, 2 * shard), jnp.float32)


def join_blocks_kernel(shard, home_ref, *refs):
    ins, out = refs[:4], refs[4]
    for kind, upward in enumerate(block_parities()):
        first, second = (rows4(ref, 0) for ref in ins[2 * kind : 2 * kind + 2])
        above = [jnp.where(upward, x, y) for x, y in zip(first, second)]
        below = [jnp.where(upward, y, x) for x, y in zip(first, second)]
        for half in range(2):
            here = slice(2 * half * shard, 2 * (half + 1) * shard)
            total = joined(rows4(home_ref, 4 * kind, here), above if half == kind else below)
            for k, value in enumerate(total):
                at = 4 * kind + k
                out[at : at + 1, here] = value


def row_factors(stat_ref, tops, index, shard):
    max_s, total_s, max_t, total_t = rows4(stat_ref, 0, pl.ds(index * shard, shard))
    sub = lax.broadcasted_iota(jnp.int32, (128, shard), 0)
    packed = jnp.zeros((128, shard), jnp.float32)
    for k, (top_s, _, top_t, _) in enumerate(tops):
        packed = jnp.where(sub == 2 * k, jnp.exp2(top_s - max_s) / total_s, packed)
        packed = jnp.where(sub == 2 * k + 1, jnp.exp2(top_t - max_t) / total_t, packed)
    packed = packed.T
    return [packed[:, k : k + 1] for k in range(2 * len(tops))]


def weigh(below, here, columns, row, tops, stats):
    row_s, col_s, row_t, col_t = (ref[here, columns] for ref in below)
    top_s, _, top_t, _ = tops
    max_s, total_s, max_t, total_t = stats
    return (
        row_s * row[0]
        - row_t * row[1]
        + col_s * (jnp.exp2(top_s - max_s) / total_s)
        - col_t * (jnp.exp2(top_t - max_t) / total_t)
    ).astype(jnp.bfloat16)


def text_term(image, weights):
    return lax.dot_general(
        image, weights, (((0,), (0,)), ((), ())), preferred_element_type=jnp.float32
    )


def image_term(weights, texts, span):
    total = None
    for index, text in enumerate(texts):
        shard = weights[0].shape[1] // 2
        part = jnp.dot(
            weights[index // 2][:, (index % 2) * shard : (index % 2 + 1) * shard],
            rows_of(text, span),
            preferred_element_type=jnp.float32,
        )
        total = part if total is None else total + part
    return total


def ahead_kernel(shard, span, *refs):
    below, refs = (refs[0:4], refs[4:8], refs[8:12], refs[12:16]), refs[16:]
    rows_in, cols_in, stat_ref = refs[0:8:2], refs[1:8:2], refs[8]
    images = (refs[9:10], refs[10:11], refs[11:13], refs[13:15])
    texts, refs = text_parts(refs[15:], 4)
    same_out, cross_out, weights_out, img_out, both_out = (
        refs[0:2], refs[2:4], refs[4], refs[5:7], refs[7]
    )
    home, third = slice(0, 2 * shard), slice(2 * shard, 3 * shard)
    fourth, far = slice(3 * shard, 4 * shard), slice(2 * shard, 4 * shard)
    col_home, col_third, col_last, col_far = (
        rows4(stat_ref, 4, at) for at in (home, third, fourth, far)
    )

    def weights_of(index):
        if index == 3:
            here = pl.ds(0, shard)
            row = row_factors(stat_ref, (rows4(rows_in[FAR], 0),), index, shard)
            weights, near = (
                weigh(below[FAR], here, at, row, rows4(cols_in[FAR], 0, at), columns)
                for at, columns in ((far, col_far), (home, col_home))
            )
            return weights, near
        call, place = (HOME, index) if index < 2 else (NEAR, 0)
        here, side = pl.ds(place * shard, shard), pl.ds(index * shard, shard)
        tops = (rows4(rows_in[call], 0, here), rows4(rows_in[SIDE], 0, side))
        row = row_factors(stat_ref, tops, index, shard)
        seen = rows4(cols_in[call], 4 * place, third)
        weights = [weigh(below[call], here, third, row[:2], seen, col_third)]
        seen = rows4(cols_in[SIDE], 4 * index)
        weights.append(weigh(below[SIDE], side, slice(None), row[2:], seen, col_last))
        near = None
        if index == 2:
            seen = rows4(cols_in[call], 4 * place, home)
            near = weigh(below[call], here, home, row[:2], seen, col_home)
        return jnp.concatenate(weights, axis=1), near

    total = both = None
    ready = weights_of(0)
    for index in range(4):
        weights, near = ready
        if index < 3:
            ready = weights_of(index + 1)
        image = rows_of(images[index], span)
        term = text_term(image, weights)
        total = total + term if index else term
        if index < 2:
            weights_out[pl.ds(index * shard, shard)] = weights
            continue
        term = text_term(image, near)
        both = term if index == 2 else both + term
        out = img_out[index - 2]
        out[...] = image_term((near, weights), texts, span).astype(out.dtype)
    height = total.shape[0] // 2
    for index in range(2):
        part = total[index * height : (index + 1) * height]
        same_out[index][...] = part[:, :shard]
        cross_out[index][...] = part[:, shard:].astype(jnp.bfloat16)
    both_out[...] = both


def home_kernel(shard, span, *refs):
    below, (row_in, col_in, stat_ref) = refs[0:4], refs[4:7]
    images = (refs[7:8], refs[8:9])
    texts, (weights_in, both_in, *outs) = text_parts(refs[9:], 4)
    img_out, txt_own, txt_x = outs[0:2], *outs[2:]
    home = slice(0, 2 * shard)
    col_home = rows4(stat_ref, 4, home)
    total = both_in[...]
    for index in range(2):
        here = pl.ds(index * shard, shard)
        row = row_factors(stat_ref, (rows4(row_in, 0, here),), index, shard)
        tops = rows4(col_in, 4 * index, home)
        weights = weigh(below, here, home, row, tops, col_home)
        total = total + text_term(rows_of(images[index], span), weights)
        out = img_out[index]
        out[...] = image_term((weights, weights_in[here]), texts, span).astype(out.dtype)
    txt_own[...] = total[:, :shard]
    txt_x[...] = total[:, shard:].astype(jnp.bfloat16)


def add_kernel(first, second, out):
    total = first[...] + second[...].astype(jnp.float32)
    out[...] = total.astype(out.dtype)


def finish_image_kernel(scale, own, core, home, out):
    total = own[...] + core[...].astype(jnp.float32)
    out[...] = (total + home[...].astype(jnp.float32)) * scale


def finish_text_kernel(scale, own, *refs):
    homes, out = refs[:-1], refs[-1]
    width = homes[0].shape[0]
    for index, home in enumerate(homes):
        here = slice(index * width, (index + 1) * width)
        total = own[here] + home[...].astype(jnp.float32)
        out[:, here] = total.T * scale


def on_device(student_image, student_text, teacher_image, teacher_text):
    shard, width_s = student_image.shape
    width_t = teacher_image.shape[1]
    scale_s = 2.0 / math.sqrt(width_s)
    scale_t = 2.0 / math.sqrt(width_t)
    f32 = jnp.float32
    bf16 = jnp.bfloat16
    vmem = pl.BlockSpec(memory_space=pltpu.VMEM)

    def params(mib):
        return pltpu.CompilerParams(vmem_limit_bytes=mib * MIB)


    spans = (slice(0, width_s), slice(width_s, width_s + width_t))
    scales = (scale_s, scale_t)

    def pack(first, second, halves, name):
        heights = (shard,) + (shard // 2,) * halves
        return pl.pallas_call(
            pack_kernel,
            out_shape=tuple(
                jax.ShapeDtypeStruct((height, width_s + width_t), bf16) for height in heights
            ),
            in_specs=[vmem] * 2,
            out_specs=(vmem,) * len(heights),
            compiler_params=params(8),
            name=name,
        )(first, second)

    text_t_ahead, text_t_x = ahead(teacher_text, -2), to_other_x(teacher_text)
    text_s_ahead, text_s_x = ahead(student_text, -2), to_other_x(student_text)
    image_s_core, image_t_core = to_other_core(student_image), to_other_core(teacher_image)
    image, top, bottom = pack(student_image, teacher_image, 2, "pack_images")
    top, image_s_core, image_t_core = lax.optimization_barrier((top, image_s_core, image_t_core))
    top = send_to(top, lambda block, x, core: (block ^ 1, x, core))
    top, bottom, late_s, late_t = lax.optimization_barrier(
        (top, bottom, text_s_ahead, text_t_ahead, text_s_x, text_t_x)
    )[:4]
    packed, first = width_s + width_t, shard // 8
    text_ahead, rest, text_x, text_part = pl.pallas_call(
        pack_arrived_kernel,
        out_shape=tuple(
            jax.ShapeDtypeStruct((height, packed), bf16)
            for height in (shard, shard - first, shard, first)
        ),
        in_specs=[vmem] * 4,
        out_specs=(vmem,) * 4,
        compiler_params=params(8),
        name="pack_arrived",
    )(late_s, late_t, text_s_x, text_t_x)
    (text,) = pack(student_text, teacher_text, 0, "pack_own")
    (image_core,) = pack(image_s_core, image_t_core, 0, "pack_core")

    def stat(shards):
        return jax.ShapeDtypeStruct((8, shards * shard), f32)

    def score(rows, columns):
        return jax.ShapeDtypeStruct((rows * shard, columns * shard), f32)

    def part_scores(shards, texts, name, cost=None):
        sizes, count = tuple(len(parts) for parts in shards), {3: 3, 2: 1, 5: 4}[len(texts)]
        outs = (score(len(sizes), count),) * 4
        outs += (stat(len(sizes)), jax.ShapeDtypeStruct((4 * len(sizes), count * shard), f32))
        args = [part for parts in shards for part in parts] + list(texts)
        *below, row, col = pl.pallas_call(
            lambda *refs: part_kernel(shard, scales, spans, sizes, count, *refs),
            out_shape=outs,
            in_specs=[vmem] * len(args),
            out_specs=(vmem,) * len(outs),
            compiler_params=params(16),
            cost_estimate=cost,
            name=name,
        )(*args)
        return below, [row, col]

    text_both = (ahead(text_part, -2), to_other_x(rest))
    top = send_to(top, lambda block, x, core: (block + 2 - block % 2 * 2, x, core))
    bottom = ahead(bottom, 1)
    texts = (text, text_x, text_ahead, *text_both)
    own = ((image,), (image_core,))
    home, home_stats = part_scores(own, texts[:3], "scores_home")
    top, bottom = lax.optimization_barrier((top, bottom, home_stats[0]))[:2]
    behind = ((top, bottom), (to_other_core(top), to_other_core(bottom)))
    near, near_stats = part_scores(behind[:1], texts[:3], "scores_near")
    side, side_stats = part_scores((*own, behind[0]), texts[3:], "scores_side", HEAVY)
    others = (*home_stats, *near_stats, *side_stats)
    *far, far_row, far_col, partial = pl.pallas_call(
        lambda *refs: far_kernel(shard, scales, spans, *refs),
        out_shape=(score(1, 4),) * 4
        + (stat(1), jax.ShapeDtypeStruct((4, 4 * shard), f32), stat(4)),
        in_specs=[vmem] * 13,
        out_specs=(vmem,) * 7,
        compiler_params=params(16),
        name="scores_far",
    )(*behind[1], *texts, *others)
    images = (image, image_core, *behind[0], *behind[1])
    calls_stats = (*others, far_row, far_col)

    shared = jax.ShapeDtypeStruct((8, 2 * shard), f32)
    group, *away = pl.pallas_call(
        lambda *refs: join_group_kernel(shard, *refs),
        out_shape=(stat(4),) + (shared,) * 4,
        in_specs=[vmem] * 3,
        out_specs=(vmem,) * 5,
        compiler_params=params(8),
        name="join_group",
    )(partial, to_other_core(partial), to_other_x(partial))
    away = [
        send_to(part, lambda block, x, core, step=step, first=first: (
            block + (step if (block // step) % 2 == first else -step), x, core
        ))
        for part, step, first in zip(away, (1, 1, 2, 2), (0, 1, 0, 1))
    ]
    stats = pl.pallas_call(
        lambda *refs: join_blocks_kernel(shard, *refs),
        out_shape=stat(4),
        in_specs=[vmem] * 5,
        out_specs=vmem,
        compiler_params=params(8),
        name="join_blocks",
    )(group, *away)

    wide = jax.ShapeDtypeStruct((shard, width_s), f32)
    tall = jax.ShapeDtypeStruct((width_s, shard), f32)
    sent = jax.ShapeDtypeStruct((width_s, shard), bf16)
    flat = jax.ShapeDtypeStruct((shard, width_s), bf16)
    tall_half = jax.ShapeDtypeStruct((width_s // 2, shard), f32)
    sent_half = jax.ShapeDtypeStruct((width_s // 2, shard), bf16)
    *txt_ahead, weights, img_back, img_cross, txt_both = pl.pallas_call(
        lambda *refs: ahead_kernel(shard, spans[0], *refs),
        out_shape=(
            tall_half,
            tall_half,
            sent_half,
            sent_half,
            jax.ShapeDtypeStruct((2 * shard, 2 * shard), bf16),
            wide,
            flat,
            jax.ShapeDtypeStruct((width_s, 2 * shard), f32),
        ),
        in_specs=[vmem] * 36,
        out_specs=(vmem,) * 8,
        compiler_params=params(24),
        name="gradients_ahead",
    )(
        *home, *near, *side, *far, *calls_stats, stats,
        *images, *texts,
    )
    img_own, img_core, txt_own, txt_x = pl.pallas_call(
        lambda *refs: home_kernel(shard, spans[0], *refs),
        out_shape=(wide, flat, tall, sent),
        in_specs=[vmem] * 16,
        out_specs=(vmem,) * 4,
        compiler_params=params(24),
        name="gradients_home",
    )(*home, *home_stats, stats, *images[:2], *texts, weights, txt_both)

    img_cross = to_other_core(img_cross)
    img_sum = (img_back + img_cross.astype(f32)).astype(bf16)
    img_home = ahead(img_sum, -1)
    txt_same, txt_cross = txt_ahead[:2], [to_other_x(part) for part in txt_ahead[2:]]
    img_core = to_other_core(img_core)

    def add(first, second, out, name):
        return pl.pallas_call(
            add_kernel,
            out_shape=out,
            in_specs=[vmem] * 2,
            out_specs=vmem,
            compiler_params=params(8),
            cost_estimate=LIGHT,
            name=name,
        )(first, second)

    txt_cross[0] = lax.optimization_barrier((txt_cross[0], img_sum))[0]
    txt_sum = add(txt_same[0], txt_cross[0], sent_half, "add_text")
    txt_x, txt_cross[1] = lax.optimization_barrier((txt_x, txt_cross[1], txt_sum))[:2]
    txt_home = [
        ahead(txt_sum, 2), ahead(add(txt_same[1], txt_cross[1], sent_half, "add_text"), 2)
    ]
    txt_own = add(txt_own, to_other_x(txt_x), tall, "add_own_text")

    def finish(kernel, *args, name):
        return pl.pallas_call(
            lambda *refs: kernel(scale_s, *refs),
            out_shape=wide,
            in_specs=[vmem] * len(args),
            out_specs=vmem,
            compiler_params=params(8),
            name=name,
        )(*args)

    grad_image = finish(finish_image_kernel, img_own, img_core, img_home, name="finish_image")
    *txt_home, txt_own, grad_image = lax.optimization_barrier((*txt_home, txt_own, grad_image))
    grad_text = finish(finish_text_kernel, txt_own, *txt_home, name="finish_text")
    return (grad_image, grad_text)


def solution(mesh):
    spec = P(AXES, None)
    return jax.shard_map(
        on_device,
        mesh=mesh,
        in_specs=(spec, spec, spec, spec),
        out_specs=(spec, spec),
        check_vma=False,
    )
```

```python
import math

import jax
import jax.numpy as jnp
from jax import lax
from jax.experimental import pallas as pl
from jax.experimental.pallas import tpu as pltpu
from jax.sharding import PartitionSpec as P

AXES = ("dp", "pair")
MIB = 1024 * 1024
LOG2E = math.log2(math.e)
HEAVY = pl.CostEstimate(flops=10**11, bytes_accessed=10**9, transcendentals=0)
LIGHT = pl.CostEstimate(flops=3 * 10**9, bytes_accessed=3 * 10**7, transcendentals=0)


def send_to(value, place):
    count = lax.axis_size("dp")
    pairs = []
    for block in range(count):
        for member in range(4):
            to_block, to_x, to_core = place(block, member // 2, member % 2)
            pairs.append((block * 4 + member, (to_block % count) * 4 + to_x * 2 + to_core))
    return lax.ppermute(value, AXES, pairs)


def to_other_core(value):
    return send_to(value, lambda block, x, core: (block, x, 1 - core))


def to_other_x(value):
    return send_to(value, lambda block, x, core: (block, 1 - x, core))


def ahead(value, steps):
    return send_to(value, lambda block, x, core: (block + steps, x, core))


def joined(first, second):
    rows = []
    for offset in (0, 2):
        rows += merged(first[offset : offset + 2], second[offset : offset + 2])
    return rows


def pack_kernel(first, second, whole, *halves):
    width = first.shape[1]
    half = first.shape[0] // 2
    whole[:, :width] = first[...]
    whole[:, width:] = second[...]
    for index, out in enumerate(halves):
        here = pl.ds(index * half, half)
        out[:, :width] = first[here]
        out[:, width:] = second[here]


def pack_arrived_kernel(s_ahead, t_ahead, s_x, t_x, ahead_out, rest_out, x_out, part_out):
    width, first = s_x.shape[1], part_out.shape[0]
    for student, teacher, whole, part, here in (
        (s_ahead, t_ahead, ahead_out, rest_out, pl.ds(first, s_x.shape[0] - first)),
        (s_x, t_x, x_out, part_out, pl.ds(0, first)),
    ):
        whole[:, :width] = student[...]
        whole[:, width:] = teacher[...]
        part[:, :width] = student[here]
        part[:, width:] = teacher[here]


def rows_of(parts, columns):
    parts = [part[:, columns] for part in parts]
    return parts[0] if len(parts) == 1 else jnp.concatenate(parts, axis=0)


def tile_of(image, texts, span, scale):
    parts = [
        lax.dot_general(
            image,
            rows_of(text, span),
            (((1,), (1,)), ((), ())),
            preferred_element_type=jnp.float32,
        )
        for text in texts
    ]
    tile = parts[0] if len(parts) == 1 else jnp.concatenate(parts, axis=1)
    return tile * (scale * LOG2E)


def stats_along(tile, axis):
    top = jnp.max(tile, axis=axis, keepdims=True)
    below = jnp.exp2(tile - top)
    return top, jnp.sum(below, axis=axis, keepdims=True), below


def merged(first, second):
    top = jnp.maximum(first[0], second[0])
    return top, first[1] * jnp.exp2(first[0] - top) + second[1] * jnp.exp2(second[0] - top)


def as_rows(columns, shard):
    lane = lax.broadcasted_iota(jnp.int32, (shard, 128), 1)
    packed = jnp.zeros((shard, 128), jnp.float32)
    for k, column in enumerate(columns):
        packed = jnp.where(lane == k, column, packed)
    return packed.T[:8]


def score_shards(images, texts, spans, scales, outs, shard):
    stats = [([], []) for _ in images]
    waiting = None
    for step in [(index, which) for index in range(len(images)) for which in range(2)] + [None]:
        tile = None
        if step:
            index, which = step
            image = rows_of(images[index], spans[which])
            tile = tile_of(image, texts, spans[which], scales[which])
        if waiting:
            (index, which), old = waiting
            here = pl.ds(index * shard, shard)
            for axis, found in ((1, stats[index][0]), (0, stats[index][1])):
                top, total, outs[2 * which + 1 - axis][here] = stats_along(old, axis)
                found += (top, total)
        waiting = step, tile
    return stats


def rows4(ref, first, columns=slice(None)):
    part = ref[first : first + 4, columns]
    return [part[k : k + 1] for k in range(4)]


def text_parts(refs, count):
    whole = count - 1
    texts = [(ref,) for ref in refs[:whole]]
    if count == 3:
        return texts + [refs[whole : whole + 1]], refs[whole + 1 :]
    return texts + [refs[whole : whole + 2]], refs[whole + 2 :]


def part_kernel(shard, scales, spans, sizes, count, *refs):
    images = []
    for size in sizes:
        images.append(refs[:size])
        refs = refs[size:]
    texts, refs = text_parts(refs, count)
    outs, (row_out, col_out) = refs[:4], refs[4:]
    stats = score_shards(images, texts, spans, scales, outs, shard)
    for index, (row, column) in enumerate(stats):
        row_out[:, pl.ds(index * shard, shard)] = as_rows(row, shard)
        for k, value in enumerate(column):
            col_out[4 * index + k : 4 * index + k + 1] = value


def far_kernel(shard, scales, spans, *refs):
    outs = refs[13:]
    part_kernel(shard, scales, spans, (2,), 4, *refs[:7], *outs[:6])
    total_kernel(shard, *refs[7:13], outs[4], outs[5], outs[6])


HOME, NEAR, SIDE, FAR = range(4)


def join_calls(rows_in, cols_in, shard):
    rows = []
    for index in range(3):
        call, place = (HOME, index) if index < 2 else (NEAR, 0)
        first = rows4(rows_in[call], 0, pl.ds(place * shard, shard))
        rows.append(joined(first, rows4(rows_in[SIDE], 0, pl.ds(index * shard, shard))))
    rows.append(rows4(rows_in[FAR], 0))
    columns = rows4(cols_in[FAR], 0)
    seen = [part[:, : 3 * shard] for part in columns]
    last = [part[:, 3 * shard :] for part in columns]
    for call, place in ((HOME, 0), (HOME, 1), (NEAR, 0)):
        seen = joined(seen, rows4(cols_in[call], 4 * place))
    for place in range(3):
        last = joined(last, rows4(cols_in[SIDE], 4 * place))
    return rows, seen, last


def total_kernel(shard, *refs):
    rows, seen, last = join_calls(refs[0:8:2], refs[1:8:2], shard)
    out = refs[8]
    for k in range(4):
        for index in range(4):
            out[k : k + 1, index * shard : (index + 1) * shard] = rows[index][k]
        out[4 + k : 5 + k, : 3 * shard] = seen[k]
        out[4 + k : 5 + k, 3 * shard :] = last[k]


def piece_stats(ref, kind, piece, shard):
    part = ref[4 * kind : 4 * kind + 4, piece * shard : (piece + 1) * shard]
    return [part[k : k + 1] for k in range(4)]


def block_parities():
    block = lax.axis_index("dp")
    return lax.rem(block, 2) == 0, lax.rem(block // 2, 2) == 0


def join_group_kernel(shard, mine_ref, core_ref, x_ref, home_ref, *outs):
    halves = []
    for kind, other_ref in enumerate((core_ref, x_ref)):
        for half in range(2):
            joint = []
            for piece in (2 * half, 2 * half + 1):
                total = joined(
                    piece_stats(mine_ref, kind, piece, shard),
                    piece_stats(other_ref, kind, piece ^ 1, shard),
                )
                for k, value in enumerate(total):
                    at = 4 * kind + k
                    home_ref[at : at + 1, piece * shard : (piece + 1) * shard] = value
                joint.append(total)
            halves.append([jnp.concatenate(pair, axis=1) for pair in zip(*joint)])
    for kind, upward in enumerate(block_parities()):
        up, down = halves[2 * kind + kind], halves[2 * kind + 1 - kind]
        for k in range(4):
            outs[2 * kind][k : k + 1] = jnp.where(upward, up[k], down[k])
            outs[2 * kind + 1][k : k + 1] = jnp.where(upward, down[k], up[k])
        for out in outs[2 * kind : 2 * kind + 2]:
            out[4:8] = jnp.zeros((4, 2 * shard), jnp.float32)


def join_blocks_kernel(shard, home_ref, *refs):
    ins, out = refs[:4], refs[4]
    for kind, upward in enumerate(block_parities()):
        first, second = (rows4(ref, 0) for ref in ins[2 * kind : 2 * kind + 2])
        above = [jnp.where(upward, x, y) for x, y in zip(first, second)]
        below = [jnp.where(upward, y, x) for x, y in zip(first, second)]
        for half in range(2):
            here = slice(2 * half * shard, 2 * (half + 1) * shard)
            total = joined(rows4(home_ref, 4 * kind, here), above if half == kind else below)
            for k, value in enumerate(total):
                at = 4 * kind + k
                out[at : at + 1, here] = value


def row_factors(stat_ref, tops, index, shard):
    max_s, total_s, max_t, total_t = rows4(stat_ref, 0, pl.ds(index * shard, shard))
    sub = lax.broadcasted_iota(jnp.int32, (128, shard), 0)
    packed = jnp.zeros((128, shard), jnp.float32)
    for k, (top_s, _, top_t, _) in enumerate(tops):
        packed = jnp.where(sub == 2 * k, jnp.exp2(top_s - max_s) / total_s, packed)
        packed = jnp.where(sub == 2 * k + 1, jnp.exp2(top_t - max_t) / total_t, packed)
    packed = packed.T
    return [packed[:, k : k + 1] for k in range(2 * len(tops))]


def weigh(below, here, columns, row, tops, stats):
    row_s, col_s, row_t, col_t = (ref[here, columns] for ref in below)
    top_s, _, top_t, _ = tops
    max_s, total_s, max_t, total_t = stats
    return (
        row_s * row[0]
        - row_t * row[1]
        + col_s * (jnp.exp2(top_s - max_s) / total_s)
        - col_t * (jnp.exp2(top_t - max_t) / total_t)
    ).astype(jnp.bfloat16)


def text_term(image, weights):
    return lax.dot_general(
        image, weights, (((0,), (0,)), ((), ())), preferred_element_type=jnp.float32
    )


def image_term(weights, texts, span):
    total = None
    for index, text in enumerate(texts):
        shard = weights[0].shape[1] // 2
        part = jnp.dot(
            weights[index // 2][:, (index % 2) * shard : (index % 2 + 1) * shard],
            rows_of(text, span),
            preferred_element_type=jnp.float32,
        )
        total = part if total is None else total + part
    return total


def ahead_kernel(shard, span, *refs):
    below, refs = (refs[0:4], refs[4:8], refs[8:12], refs[12:16]), refs[16:]
    rows_in, cols_in, stat_ref = refs[0:8:2], refs[1:8:2], refs[8]
    images = (refs[9:10], refs[10:11], refs[11:13], refs[13:15])
    texts, refs = text_parts(refs[15:], 4)
    same_out, cross_out, weights_out, img_out, both_out = (
        refs[0:2], refs[2:4], refs[4], refs[5:7], refs[7]
    )
    home, third = slice(0, 2 * shard), slice(2 * shard, 3 * shard)
    fourth, far = slice(3 * shard, 4 * shard), slice(2 * shard, 4 * shard)
    col_home, col_third, col_last, col_far = (
        rows4(stat_ref, 4, at) for at in (home, third, fourth, far)
    )

    def weights_of(index):
        if index == 3:
            here = pl.ds(0, shard)
            row = row_factors(stat_ref, (rows4(rows_in[FAR], 0),), index, shard)
            weights, near = (
                weigh(below[FAR], here, at, row, rows4(cols_in[FAR], 0, at), columns)
                for at, columns in ((far, col_far), (home, col_home))
            )
            return weights, near
        call, place = (HOME, index) if index < 2 else (NEAR, 0)
        here, side = pl.ds(place * shard, shard), pl.ds(index * shard, shard)
        tops = (rows4(rows_in[call], 0, here), rows4(rows_in[SIDE], 0, side))
        row = row_factors(stat_ref, tops, index, shard)
        seen = rows4(cols_in[call], 4 * place, third)
        weights = [weigh(below[call], here, third, row[:2], seen, col_third)]
        seen = rows4(cols_in[SIDE], 4 * index)
        weights.append(weigh(below[SIDE], side, slice(None), row[2:], seen, col_last))
        near = None
        if index == 2:
            seen = rows4(cols_in[call], 4 * place, home)
            near = weigh(below[call], here, home, row[:2], seen, col_home)
        return jnp.concatenate(weights, axis=1), near

    total = both = None
    ready = weights_of(0)
    for index in range(4):
        weights, near = ready
        if index < 3:
            ready = weights_of(index + 1)
        image = rows_of(images[index], span)
        term = text_term(image, weights)
        total = total + term if index else term
        if index < 2:
            weights_out[pl.ds(index * shard, shard)] = weights
            continue
        term = text_term(image, near)
        both = term if index == 2 else both + term
        out = img_out[index - 2]
        out[...] = image_term((near, weights), texts, span).astype(out.dtype)
    height = total.shape[0] // 2
    for index in range(2):
        part = total[index * height : (index + 1) * height]
        same_out[index][...] = part[:, :shard]
        cross_out[index][...] = part[:, shard:].astype(jnp.bfloat16)
    both_out[...] = both


def home_kernel(shard, span, *refs):
    below, (row_in, col_in, stat_ref) = refs[0:4], refs[4:7]
    images = (refs[7:8], refs[8:9])
    texts, (weights_in, both_in, *outs) = text_parts(refs[9:], 4)
    img_out, txt_own, txt_x = outs[0:2], *outs[2:]
    home = slice(0, 2 * shard)
    col_home = rows4(stat_ref, 4, home)
    total = both_in[...]
    for index in range(2):
        here = pl.ds(index * shard, shard)
        row = row_factors(stat_ref, (rows4(row_in, 0, here),), index, shard)
        tops = rows4(col_in, 4 * index, home)
        weights = weigh(below, here, home, row, tops, col_home)
        total = total + text_term(rows_of(images[index], span), weights)
        out = img_out[index]
        out[...] = image_term((weights, weights_in[here]), texts, span).astype(out.dtype)
    txt_own[...] = total[:, :shard]
    txt_x[...] = total[:, shard:].astype(jnp.bfloat16)


def add_kernel(first, second, out):
    total = first[...] + second[...].astype(jnp.float32)
    out[...] = total.astype(out.dtype)


def finish_image_kernel(scale, own, core, home, out):
    total = own[...] + core[...].astype(jnp.float32)
    out[...] = (total + home[...].astype(jnp.float32)) * scale


def finish_text_kernel(scale, own, *refs):
    homes, out = refs[:-1], refs[-1]
    width = homes[0].shape[0]
    for index, home in enumerate(homes):
        here = slice(index * width, (index + 1) * width)
        total = own[here] + home[...].astype(jnp.float32)
        out[:, here] = total.T * scale


def on_device(student_image, student_text, teacher_image, teacher_text):
    shard, width_s = student_image.shape
    width_t = teacher_image.shape[1]
    scale_s = 2.0 / math.sqrt(width_s)
    scale_t = 2.0 / math.sqrt(width_t)
    f32 = jnp.float32
    bf16 = jnp.bfloat16
    vmem = pl.BlockSpec(memory_space=pltpu.VMEM)

    def params(mib):
        return pltpu.CompilerParams(vmem_limit_bytes=mib * MIB)


    spans = (slice(0, width_s), slice(width_s, width_s + width_t))
    scales = (scale_s, scale_t)

    def pack(first, second, halves, name):
        heights = (shard,) + (shard // 2,) * halves
        return pl.pallas_call(
            pack_kernel,
            out_shape=tuple(
                jax.ShapeDtypeStruct((height, width_s + width_t), bf16) for height in heights
            ),
            in_specs=[vmem] * 2,
            out_specs=(vmem,) * len(heights),
            compiler_params=params(8),
            name=name,
        )(first, second)

    text_t_ahead, text_t_x = ahead(teacher_text, -2), to_other_x(teacher_text)
    text_s_ahead, text_s_x = ahead(student_text, -2), to_other_x(student_text)
    image_s_core, image_t_core = to_other_core(student_image), to_other_core(teacher_image)
    image, top, bottom = pack(student_image, teacher_image, 2, "pack_images")
    bottom, image_s_core, image_t_core = lax.optimization_barrier(
        (bottom, image_s_core, image_t_core)
    )
    bottom = send_to(bottom, lambda block, x, core: (block ^ 1, x, core))
    top, bottom, late_s, late_t = lax.optimization_barrier(
        (top, bottom, text_s_ahead, text_t_ahead, text_s_x, text_t_x)
    )[:4]
    packed, first = width_s + width_t, shard // 8
    text_ahead, rest, text_x, text_part = pl.pallas_call(
        pack_arrived_kernel,
        out_shape=tuple(
            jax.ShapeDtypeStruct((height, packed), bf16)
            for height in (shard, shard - first, shard, first)
        ),
        in_specs=[vmem] * 4,
        out_specs=(vmem,) * 4,
        compiler_params=params(8),
        name="pack_arrived",
    )(late_s, late_t, text_s_x, text_t_x)
    (text,) = pack(student_text, teacher_text, 0, "pack_own")
    (image_core,) = pack(image_s_core, image_t_core, 0, "pack_core")

    def stat(shards):
        return jax.ShapeDtypeStruct((8, shards * shard), f32)

    def score(rows, columns):
        return jax.ShapeDtypeStruct((rows * shard, columns * shard), f32)

    def part_scores(shards, texts, name, cost=None):
        sizes, count = tuple(len(parts) for parts in shards), {3: 3, 2: 1, 5: 4}[len(texts)]
        outs = (score(len(sizes), count),) * 4
        outs += (stat(len(sizes)), jax.ShapeDtypeStruct((4 * len(sizes), count * shard), f32))
        args = [part for parts in shards for part in parts] + list(texts)
        *below, row, col = pl.pallas_call(
            lambda *refs: part_kernel(shard, scales, spans, sizes, count, *refs),
            out_shape=outs,
            in_specs=[vmem] * len(args),
            out_specs=(vmem,) * len(outs),
            compiler_params=params(16),
            cost_estimate=cost,
            name=name,
        )(*args)
        return below, [row, col]

    text_both = (ahead(text_part, -2), to_other_x(rest))
    top = ahead(top, 1)
    bottom = send_to(bottom, lambda block, x, core: (block + 2 - block % 2 * 2, x, core))
    texts = (text, text_x, text_ahead, *text_both)
    own = ((image,), (image_core,))
    home, home_stats = part_scores(own, texts[:3], "scores_home")
    top, bottom = lax.optimization_barrier((top, bottom, home_stats[0]))[:2]
    behind = ((top, bottom), (to_other_core(top), to_other_core(bottom)))
    near, near_stats = part_scores(behind[:1], texts[:3], "scores_near")
    side, side_stats = part_scores((*own, behind[0]), texts[3:], "scores_side", HEAVY)
    others = (*home_stats, *near_stats, *side_stats)
    *far, far_row, far_col, partial = pl.pallas_call(
        lambda *refs: far_kernel(shard, scales, spans, *refs),
        out_shape=(score(1, 4),) * 4
        + (stat(1), jax.ShapeDtypeStruct((4, 4 * shard), f32), stat(4)),
        in_specs=[vmem] * 13,
        out_specs=(vmem,) * 7,
        compiler_params=params(16),
        name="scores_far",
    )(*behind[1], *texts, *others)
    images = (image, image_core, *behind[0], *behind[1])
    calls_stats = (*others, far_row, far_col)

    shared = jax.ShapeDtypeStruct((8, 2 * shard), f32)
    group, *away = pl.pallas_call(
        lambda *refs: join_group_kernel(shard, *refs),
        out_shape=(stat(4),) + (shared,) * 4,
        in_specs=[vmem] * 3,
        out_specs=(vmem,) * 5,
        compiler_params=params(8),
        name="join_group",
    )(partial, to_other_core(partial), to_other_x(partial))
    away = [
        send_to(part, lambda block, x, core, step=step, first=first: (
            block + (step if (block // step) % 2 == first else -step), x, core
        ))
        for part, step, first in zip(away, (1, 1, 2, 2), (0, 1, 0, 1))
    ]
    stats = pl.pallas_call(
        lambda *refs: join_blocks_kernel(shard, *refs),
        out_shape=stat(4),
        in_specs=[vmem] * 5,
        out_specs=vmem,
        compiler_params=params(8),
        name="join_blocks",
    )(group, *away)

    wide = jax.ShapeDtypeStruct((shard, width_s), f32)
    tall = jax.ShapeDtypeStruct((width_s, shard), f32)
    sent = jax.ShapeDtypeStruct((width_s, shard), bf16)
    flat = jax.ShapeDtypeStruct((shard, width_s), bf16)
    tall_half = jax.ShapeDtypeStruct((width_s // 2, shard), f32)
    sent_half = jax.ShapeDtypeStruct((width_s // 2, shard), bf16)
    *txt_ahead, weights, img_back, img_cross, txt_both = pl.pallas_call(
        lambda *refs: ahead_kernel(shard, spans[0], *refs),
        out_shape=(
            tall_half,
            tall_half,
            sent_half,
            sent_half,
            jax.ShapeDtypeStruct((2 * shard, 2 * shard), bf16),
            wide,
            flat,
            jax.ShapeDtypeStruct((width_s, 2 * shard), f32),
        ),
        in_specs=[vmem] * 36,
        out_specs=(vmem,) * 8,
        compiler_params=params(24),
        name="gradients_ahead",
    )(
        *home, *near, *side, *far, *calls_stats, stats,
        *images, *texts,
    )
    img_own, img_core, txt_own, txt_x = pl.pallas_call(
        lambda *refs: home_kernel(shard, spans[0], *refs),
        out_shape=(wide, flat, tall, sent),
        in_specs=[vmem] * 16,
        out_specs=(vmem,) * 4,
        compiler_params=params(24),
        name="gradients_home",
    )(*home, *home_stats, stats, *images[:2], *texts, weights, txt_both)

    img_cross = to_other_core(img_cross)
    img_sum = (img_back + img_cross.astype(f32)).astype(bf16)
    img_home = ahead(img_sum, -1)
    txt_same, txt_cross = txt_ahead[:2], [to_other_x(part) for part in txt_ahead[2:]]
    img_core = to_other_core(img_core)

    def add(first, second, out, name):
        return pl.pallas_call(
            add_kernel,
            out_shape=out,
            in_specs=[vmem] * 2,
            out_specs=vmem,
            compiler_params=params(8),
            cost_estimate=LIGHT,
            name=name,
        )(first, second)

    txt_cross[0] = lax.optimization_barrier((txt_cross[0], img_sum))[0]
    txt_sum = add(txt_same[0], txt_cross[0], sent_half, "add_text")
    txt_x, txt_cross[1] = lax.optimization_barrier((txt_x, txt_cross[1], txt_sum))[:2]
    txt_home = [
        ahead(txt_sum, 2), ahead(add(txt_same[1], txt_cross[1], sent_half, "add_text"), 2)
    ]
    txt_own = add(txt_own, to_other_x(txt_x), tall, "add_own_text")

    def finish(kernel, *args, name):
        return pl.pallas_call(
            lambda *refs: kernel(scale_s, *refs),
            out_shape=wide,
            in_specs=[vmem] * len(args),
            out_specs=vmem,
            compiler_params=params(8),
            name=name,
        )(*args)

    grad_image = finish(finish_image_kernel, img_own, img_core, img_home, name="finish_image")
    *txt_home, txt_own, grad_image = lax.optimization_barrier((*txt_home, txt_own, grad_image))
    grad_text = finish(finish_text_kernel, txt_own, *txt_home, name="finish_text")
    return (grad_image, grad_text)


def solution(mesh):
    spec = P(AXES, None)
    return jax.shard_map(
        on_device,
        mesh=mesh,
        in_specs=(spec, spec, spec, spec),
        out_specs=(spec, spec),
        check_vma=False,
    )
```

```python
import math

import jax
import jax.numpy as jnp
from jax import lax
from jax.experimental import pallas as pl
from jax.experimental.pallas import tpu as pltpu
from jax.sharding import PartitionSpec as P

AXES = ("dp", "pair")
MIB = 1024 * 1024
LOG2E = math.log2(math.e)
HEAVY = pl.CostEstimate(flops=10**11, bytes_accessed=10**9, transcendentals=0)
LIGHT = pl.CostEstimate(flops=3 * 10**9, bytes_accessed=3 * 10**7, transcendentals=0)


def send_to(value, place):
    count = lax.axis_size("dp")
    pairs = []
    for block in range(count):
        for member in range(4):
            to_block, to_x, to_core = place(block, member // 2, member % 2)
            pairs.append((block * 4 + member, (to_block % count) * 4 + to_x * 2 + to_core))
    return lax.ppermute(value, AXES, pairs)


def to_other_core(value):
    return send_to(value, lambda block, x, core: (block, x, 1 - core))


def to_other_x(value):
    return send_to(value, lambda block, x, core: (block, 1 - x, core))


def ahead(value, steps):
    return send_to(value, lambda block, x, core: (block + steps, x, core))


def joined(first, second):
    rows = []
    for offset in (0, 2):
        rows += merged(first[offset : offset + 2], second[offset : offset + 2])
    return rows


def pack_kernel(first, second, whole, *parts):
    width = first.shape[1]
    whole[:, :width] = first[...]
    whole[:, width:] = second[...]
    start = 0
    for out in parts:
        here = pl.ds(start, out.shape[0])
        out[:, :width] = first[here]
        out[:, width:] = second[here]
        start += out.shape[0]


def pack_arrived_kernel(s_ahead, t_ahead, s_x, t_x, ahead_out, rest_out, x_out, part_out):
    width, first = s_x.shape[1], part_out.shape[0]
    for student, teacher, whole, part, here in (
        (s_ahead, t_ahead, ahead_out, rest_out, pl.ds(first, s_x.shape[0] - first)),
        (s_x, t_x, x_out, part_out, pl.ds(0, first)),
    ):
        whole[:, :width] = student[...]
        whole[:, width:] = teacher[...]
        part[:, :width] = student[here]
        part[:, width:] = teacher[here]


def rows_of(parts, columns):
    parts = [part[:, columns] for part in parts]
    return parts[0] if len(parts) == 1 else jnp.concatenate(parts, axis=0)


def tile_of(image, texts, span, scale):
    parts = [
        lax.dot_general(
            image,
            rows_of(text, span),
            (((1,), (1,)), ((), ())),
            preferred_element_type=jnp.float32,
        )
        for text in texts
    ]
    tile = parts[0] if len(parts) == 1 else jnp.concatenate(parts, axis=1)
    return tile * (scale * LOG2E)


def stats_along(tile, axis):
    top = jnp.max(tile, axis=axis, keepdims=True)
    below = jnp.exp2(tile - top)
    return top, jnp.sum(below, axis=axis, keepdims=True), below


def merged(first, second):
    top = jnp.maximum(first[0], second[0])
    return top, first[1] * jnp.exp2(first[0] - top) + second[1] * jnp.exp2(second[0] - top)


def as_rows(columns, shard):
    lane = lax.broadcasted_iota(jnp.int32, (shard, 128), 1)
    packed = jnp.zeros((shard, 128), jnp.float32)
    for k, column in enumerate(columns):
        packed = jnp.where(lane == k, column, packed)
    return packed.T[:8]


def score_shards(images, texts, spans, scales, outs, shard):
    stats = [([], []) for _ in images]
    waiting = None
    for step in [(index, which) for index in range(len(images)) for which in range(2)] + [None]:
        tile = None
        if step:
            index, which = step
            image = rows_of(images[index], spans[which])
            tile = tile_of(image, texts, spans[which], scales[which])
        if waiting:
            (index, which), old = waiting
            here = pl.ds(index * shard, shard)
            for axis, found in ((1, stats[index][0]), (0, stats[index][1])):
                top, total, outs[2 * which + 1 - axis][here] = stats_along(old, axis)
                found += (top, total)
        waiting = step, tile
    return stats


def rows4(ref, first, columns=slice(None)):
    part = ref[first : first + 4, columns]
    return [part[k : k + 1] for k in range(4)]


def text_parts(refs, count):
    whole = count - 1
    texts = [(ref,) for ref in refs[:whole]]
    if count == 3:
        return texts + [refs[whole : whole + 1]], refs[whole + 1 :]
    return texts + [refs[whole : whole + 2]], refs[whole + 2 :]


def part_kernel(shard, scales, spans, sizes, count, *refs):
    images = []
    for size in sizes:
        images.append(refs[:size])
        refs = refs[size:]
    texts, refs = text_parts(refs, count)
    outs, (row_out, col_out) = refs[:4], refs[4:]
    stats = score_shards(images, texts, spans, scales, outs, shard)
    for index, (row, column) in enumerate(stats):
        row_out[:, pl.ds(index * shard, shard)] = as_rows(row, shard)
        for k, value in enumerate(column):
            col_out[4 * index + k : 4 * index + k + 1] = value


def far_kernel(shard, scales, spans, *refs):
    outs = refs[13:]
    part_kernel(shard, scales, spans, (2,), 4, *refs[:7], *outs[:6])
    total_kernel(shard, *refs[7:13], outs[4], outs[5], outs[6])


HOME, NEAR, SIDE, FAR = range(4)


def join_calls(rows_in, cols_in, shard):
    rows = []
    for index in range(3):
        call, place = (HOME, index) if index < 2 else (NEAR, 0)
        first = rows4(rows_in[call], 0, pl.ds(place * shard, shard))
        rows.append(joined(first, rows4(rows_in[SIDE], 0, pl.ds(index * shard, shard))))
    rows.append(rows4(rows_in[FAR], 0))
    columns = rows4(cols_in[FAR], 0)
    seen = [part[:, : 3 * shard] for part in columns]
    last = [part[:, 3 * shard :] for part in columns]
    for call, place in ((HOME, 0), (HOME, 1), (NEAR, 0)):
        seen = joined(seen, rows4(cols_in[call], 4 * place))
    for place in range(3):
        last = joined(last, rows4(cols_in[SIDE], 4 * place))
    return rows, seen, last


def total_kernel(shard, *refs):
    rows, seen, last = join_calls(refs[0:8:2], refs[1:8:2], shard)
    out = refs[8]
    for k in range(4):
        for index in range(4):
            out[k : k + 1, index * shard : (index + 1) * shard] = rows[index][k]
        out[4 + k : 5 + k, : 3 * shard] = seen[k]
        out[4 + k : 5 + k, 3 * shard :] = last[k]


def piece_stats(ref, kind, piece, shard):
    part = ref[4 * kind : 4 * kind + 4, piece * shard : (piece + 1) * shard]
    return [part[k : k + 1] for k in range(4)]


def block_parities():
    block = lax.axis_index("dp")
    return lax.rem(block, 2) == 0, lax.rem(block // 2, 2) == 0


def join_group_kernel(shard, mine_ref, core_ref, x_ref, home_ref, *outs):
    halves = []
    for kind, other_ref in enumerate((core_ref, x_ref)):
        for half in range(2):
            joint = []
            for piece in (2 * half, 2 * half + 1):
                total = joined(
                    piece_stats(mine_ref, kind, piece, shard),
                    piece_stats(other_ref, kind, piece ^ 1, shard),
                )
                for k, value in enumerate(total):
                    at = 4 * kind + k
                    home_ref[at : at + 1, piece * shard : (piece + 1) * shard] = value
                joint.append(total)
            halves.append([jnp.concatenate(pair, axis=1) for pair in zip(*joint)])
    for kind, upward in enumerate(block_parities()):
        up, down = halves[2 * kind + kind], halves[2 * kind + 1 - kind]
        for k in range(4):
            outs[2 * kind][k : k + 1] = jnp.where(upward, up[k], down[k])
            outs[2 * kind + 1][k : k + 1] = jnp.where(upward, down[k], up[k])
        for out in outs[2 * kind : 2 * kind + 2]:
            out[4:8] = jnp.zeros((4, 2 * shard), jnp.float32)


def join_blocks_kernel(shard, home_ref, *refs):
    ins, out = refs[:4], refs[4]
    for kind, upward in enumerate(block_parities()):
        first, second = (rows4(ref, 0) for ref in ins[2 * kind : 2 * kind + 2])
        above = [jnp.where(upward, x, y) for x, y in zip(first, second)]
        below = [jnp.where(upward, y, x) for x, y in zip(first, second)]
        for half in range(2):
            here = slice(2 * half * shard, 2 * (half + 1) * shard)
            total = joined(rows4(home_ref, 4 * kind, here), above if half == kind else below)
            for k, value in enumerate(total):
                at = 4 * kind + k
                out[at : at + 1, here] = value


def row_factors(stat_ref, tops, index, shard):
    max_s, total_s, max_t, total_t = rows4(stat_ref, 0, pl.ds(index * shard, shard))
    sub = lax.broadcasted_iota(jnp.int32, (128, shard), 0)
    packed = jnp.zeros((128, shard), jnp.float32)
    for k, (top_s, _, top_t, _) in enumerate(tops):
        packed = jnp.where(sub == 2 * k, jnp.exp2(top_s - max_s) / total_s, packed)
        packed = jnp.where(sub == 2 * k + 1, jnp.exp2(top_t - max_t) / total_t, packed)
    packed = packed.T
    return [packed[:, k : k + 1] for k in range(2 * len(tops))]


def weigh(below, here, columns, row, tops, stats):
    row_s, col_s, row_t, col_t = (ref[here, columns] for ref in below)
    top_s, _, top_t, _ = tops
    max_s, total_s, max_t, total_t = stats
    return (
        row_s * row[0]
        - row_t * row[1]
        + col_s * (jnp.exp2(top_s - max_s) / total_s)
        - col_t * (jnp.exp2(top_t - max_t) / total_t)
    ).astype(jnp.bfloat16)


def text_term(image, weights):
    return lax.dot_general(
        image, weights, (((0,), (0,)), ((), ())), preferred_element_type=jnp.float32
    )


def image_term(weights, texts, span):
    total = None
    for index, text in enumerate(texts):
        shard = weights[0].shape[1] // 2
        part = jnp.dot(
            weights[index // 2][:, (index % 2) * shard : (index % 2 + 1) * shard],
            rows_of(text, span),
            preferred_element_type=jnp.float32,
        )
        total = part if total is None else total + part
    return total


def ahead_kernel(shard, span, *refs):
    below, refs = (refs[0:4], refs[4:8], refs[8:12], refs[12:16]), refs[16:]
    rows_in, cols_in, stat_ref = refs[0:8:2], refs[1:8:2], refs[8]
    images = (refs[9:10], refs[10:11], refs[11:13], refs[13:15])
    texts, refs = text_parts(refs[15:], 4)
    same_out, cross_out, weights_out, img_out, both_out = (
        refs[0:2], refs[2:4], refs[4], refs[5:7], refs[7]
    )
    home, third = slice(0, 2 * shard), slice(2 * shard, 3 * shard)
    fourth, far = slice(3 * shard, 4 * shard), slice(2 * shard, 4 * shard)
    col_home, col_third, col_last, col_far = (
        rows4(stat_ref, 4, at) for at in (home, third, fourth, far)
    )

    def weights_of(index):
        if index == 3:
            here = pl.ds(0, shard)
            row = row_factors(stat_ref, (rows4(rows_in[FAR], 0),), index, shard)
            weights, near = (
                weigh(below[FAR], here, at, row, rows4(cols_in[FAR], 0, at), columns)
                for at, columns in ((far, col_far), (home, col_home))
            )
            return weights, near
        call, place = (HOME, index) if index < 2 else (NEAR, 0)
        here, side = pl.ds(place * shard, shard), pl.ds(index * shard, shard)
        tops = (rows4(rows_in[call], 0, here), rows4(rows_in[SIDE], 0, side))
        row = row_factors(stat_ref, tops, index, shard)
        seen = rows4(cols_in[call], 4 * place, third)
        weights = [weigh(below[call], here, third, row[:2], seen, col_third)]
        seen = rows4(cols_in[SIDE], 4 * index)
        weights.append(weigh(below[SIDE], side, slice(None), row[2:], seen, col_last))
        near = None
        if index == 2:
            seen = rows4(cols_in[call], 4 * place, home)
            near = weigh(below[call], here, home, row[:2], seen, col_home)
        return jnp.concatenate(weights, axis=1), near

    total = both = None
    ready = weights_of(0)
    for index in range(4):
        weights, near = ready
        if index < 3:
            ready = weights_of(index + 1)
        image = rows_of(images[index], span)
        term = text_term(image, weights)
        total = total + term if index else term
        if index < 2:
            weights_out[pl.ds(index * shard, shard)] = weights
            continue
        term = text_term(image, near)
        both = term if index == 2 else both + term
        out = img_out[index - 2]
        out[...] = image_term((near, weights), texts, span).astype(out.dtype)
    height = total.shape[0] // 2
    for index in range(2):
        part = total[index * height : (index + 1) * height]
        same_out[index][...] = part[:, :shard]
        cross_out[index][...] = part[:, shard:].astype(jnp.bfloat16)
    both_out[...] = both


def home_kernel(shard, span, *refs):
    below, (row_in, col_in, stat_ref) = refs[0:4], refs[4:7]
    images = (refs[7:8], refs[8:9])
    texts, (weights_in, both_in, *outs) = text_parts(refs[9:], 4)
    img_out, txt_own, txt_x = outs[0:2], *outs[2:]
    home = slice(0, 2 * shard)
    col_home = rows4(stat_ref, 4, home)
    total = both_in[...]
    for index in range(2):
        here = pl.ds(index * shard, shard)
        row = row_factors(stat_ref, (rows4(row_in, 0, here),), index, shard)
        tops = rows4(col_in, 4 * index, home)
        weights = weigh(below, here, home, row, tops, col_home)
        total = total + text_term(rows_of(images[index], span), weights)
        out = img_out[index]
        out[...] = image_term((weights, weights_in[here]), texts, span).astype(out.dtype)
    txt_own[...] = total[:, :shard]
    txt_x[...] = total[:, shard:].astype(jnp.bfloat16)


def add_kernel(first, second, out):
    total = first[...] + second[...].astype(jnp.float32)
    out[...] = total.astype(out.dtype)


def finish_image_kernel(scale, own, core, home, out):
    total = own[...] + core[...].astype(jnp.float32)
    out[...] = (total + home[...].astype(jnp.float32)) * scale


def finish_text_kernel(scale, own, *refs):
    homes, out = refs[:-1], refs[-1]
    width = homes[0].shape[0]
    for index, home in enumerate(homes):
        here = slice(index * width, (index + 1) * width)
        total = own[here] + home[...].astype(jnp.float32)
        out[:, here] = total.T * scale


def on_device(student_image, student_text, teacher_image, teacher_text):
    shard, width_s = student_image.shape
    width_t = teacher_image.shape[1]
    scale_s = 2.0 / math.sqrt(width_s)
    scale_t = 2.0 / math.sqrt(width_t)
    f32 = jnp.float32
    bf16 = jnp.bfloat16
    vmem = pl.BlockSpec(memory_space=pltpu.VMEM)

    def params(mib):
        return pltpu.CompilerParams(vmem_limit_bytes=mib * MIB)


    spans = (slice(0, width_s), slice(width_s, width_s + width_t))
    scales = (scale_s, scale_t)

    def pack(first, second, *heights, name):
        heights = (shard, *heights)
        return pl.pallas_call(
            pack_kernel,
            out_shape=tuple(
                jax.ShapeDtypeStruct((height, width_s + width_t), bf16) for height in heights
            ),
            in_specs=[vmem] * 2,
            out_specs=(vmem,) * len(heights),
            compiler_params=params(8),
            name=name,
        )(first, second)

    text_t_ahead, text_t_x = ahead(teacher_text, -2), to_other_x(teacher_text)
    image_s_core, image_t_core = to_other_core(student_image), to_other_core(teacher_image)
    image, top, bottom = pack(
        student_image, teacher_image, shard * 9 // 16, shard * 7 // 16, name="pack_images"
    )
    bottom = send_to(bottom, lambda block, x, core: (block ^ 1, x, core))
    late_s, image_s_core, image_t_core = lax.optimization_barrier(
        (student_text, image_s_core, image_t_core)
    )
    text_s_ahead, text_s_x = ahead(late_s, -2), to_other_x(late_s)
    top, bottom, late_s, late_t = lax.optimization_barrier(
        (top, bottom, text_s_ahead, text_t_ahead, text_s_x, text_t_x)
    )[:4]
    packed, first = width_s + width_t, shard // 8
    text_ahead, rest, text_x, text_part = pl.pallas_call(
        pack_arrived_kernel,
        out_shape=tuple(
            jax.ShapeDtypeStruct((height, packed), bf16)
            for height in (shard, shard - first, shard, first)
        ),
        in_specs=[vmem] * 4,
        out_specs=(vmem,) * 4,
        compiler_params=params(8),
        name="pack_arrived",
    )(late_s, late_t, text_s_x, text_t_x)
    (text,) = pack(student_text, teacher_text, name="pack_own")
    (image_core,) = pack(image_s_core, image_t_core, name="pack_core")

    def stat(shards):
        return jax.ShapeDtypeStruct((8, shards * shard), f32)

    def score(rows, columns):
        return jax.ShapeDtypeStruct((rows * shard, columns * shard), f32)

    def part_scores(shards, texts, name, cost=None):
        sizes, count = tuple(len(parts) for parts in shards), {3: 3, 2: 1, 5: 4}[len(texts)]
        outs = (score(len(sizes), count),) * 4
        outs += (stat(len(sizes)), jax.ShapeDtypeStruct((4 * len(sizes), count * shard), f32))
        args = [part for parts in shards for part in parts] + list(texts)
        *below, row, col = pl.pallas_call(
            lambda *refs: part_kernel(shard, scales, spans, sizes, count, *refs),
            out_shape=outs,
            in_specs=[vmem] * len(args),
            out_specs=(vmem,) * len(outs),
            compiler_params=params(16),
            cost_estimate=cost,
            name=name,
        )(*args)
        return below, [row, col]

    text_both = (ahead(text_part, -2), to_other_x(rest))
    top = ahead(top, 1)
    bottom = send_to(bottom, lambda block, x, core: (block + 2 - block % 2 * 2, x, core))
    texts = (text, text_x, text_ahead, *text_both)
    own = ((image,), (image_core,))
    home, home_stats = part_scores(own, texts[:3], "scores_home")
    top, bottom = lax.optimization_barrier((top, bottom, home_stats[0]))[:2]
    behind = ((top, bottom), (to_other_core(top), to_other_core(bottom)))
    near, near_stats = part_scores(behind[:1], texts[:3], "scores_near")
    side, side_stats = part_scores((*own, behind[0]), texts[3:], "scores_side", HEAVY)
    others = (*home_stats, *near_stats, *side_stats)
    *far, far_row, far_col, partial = pl.pallas_call(
        lambda *refs: far_kernel(shard, scales, spans, *refs),
        out_shape=(score(1, 4),) * 4
        + (stat(1), jax.ShapeDtypeStruct((4, 4 * shard), f32), stat(4)),
        in_specs=[vmem] * 13,
        out_specs=(vmem,) * 7,
        compiler_params=params(16),
        name="scores_far",
    )(*behind[1], *texts, *others)
    images = (image, image_core, *behind[0], *behind[1])
    calls_stats = (*others, far_row, far_col)

    shared = jax.ShapeDtypeStruct((8, 2 * shard), f32)
    group, *away = pl.pallas_call(
        lambda *refs: join_group_kernel(shard, *refs),
        out_shape=(stat(4),) + (shared,) * 4,
        in_specs=[vmem] * 3,
        out_specs=(vmem,) * 5,
        compiler_params=params(8),
        name="join_group",
    )(partial, to_other_core(partial), to_other_x(partial))
    away = [
        send_to(part, lambda block, x, core, step=step, first=first: (
            block + (step if (block // step) % 2 == first else -step), x, core
        ))
        for part, step, first in zip(away, (1, 1, 2, 2), (0, 1, 0, 1))
    ]
    stats = pl.pallas_call(
        lambda *refs: join_blocks_kernel(shard, *refs),
        out_shape=stat(4),
        in_specs=[vmem] * 5,
        out_specs=vmem,
        compiler_params=params(8),
        name="join_blocks",
    )(group, *away)

    wide = jax.ShapeDtypeStruct((shard, width_s), f32)
    tall = jax.ShapeDtypeStruct((width_s, shard), f32)
    sent = jax.ShapeDtypeStruct((width_s, shard), bf16)
    flat = jax.ShapeDtypeStruct((shard, width_s), bf16)
    tall_half = jax.ShapeDtypeStruct((width_s // 2, shard), f32)
    sent_half = jax.ShapeDtypeStruct((width_s // 2, shard), bf16)
    *txt_ahead, weights, img_back, img_cross, txt_both = pl.pallas_call(
        lambda *refs: ahead_kernel(shard, spans[0], *refs),
        out_shape=(
            tall_half,
            tall_half,
            sent_half,
            sent_half,
            jax.ShapeDtypeStruct((2 * shard, 2 * shard), bf16),
            wide,
            flat,
            jax.ShapeDtypeStruct((width_s, 2 * shard), f32),
        ),
        in_specs=[vmem] * 36,
        out_specs=(vmem,) * 8,
        compiler_params=params(24),
        name="gradients_ahead",
    )(
        *home, *near, *side, *far, *calls_stats, stats,
        *images, *texts,
    )
    img_cross = to_other_core(img_cross)
    img_sum = (img_back + img_cross.astype(f32)).astype(bf16)
    img_home = ahead(img_sum, -1)
    weights = lax.optimization_barrier((weights, img_sum))[0]
    img_own, img_core, txt_own, txt_x = pl.pallas_call(
        lambda *refs: home_kernel(shard, spans[0], *refs),
        out_shape=(wide, flat, tall, sent),
        in_specs=[vmem] * 16,
        out_specs=(vmem,) * 4,
        compiler_params=params(24),
        name="gradients_home",
    )(*home, *home_stats, stats, *images[:2], *texts, weights, txt_both)

    txt_same, txt_cross = txt_ahead[:2], [to_other_x(part) for part in txt_ahead[2:]]
    img_core = to_other_core(img_core)

    def add(first, second, out, name):
        return pl.pallas_call(
            add_kernel,
            out_shape=out,
            in_specs=[vmem] * 2,
            out_specs=vmem,
            compiler_params=params(8),
            cost_estimate=LIGHT,
            name=name,
        )(first, second)

    txt_cross[0] = lax.optimization_barrier((txt_cross[0], img_sum))[0]
    txt_sum = add(txt_same[0], txt_cross[0], sent_half, "add_text")
    txt_x, txt_cross[1] = lax.optimization_barrier((txt_x, txt_cross[1], txt_sum))[:2]
    txt_home = [
        ahead(txt_sum, 2), ahead(add(txt_same[1], txt_cross[1], sent_half, "add_text"), 2)
    ]
    txt_own = add(txt_own, to_other_x(txt_x), tall, "add_own_text")

    def finish(kernel, *args, name):
        return pl.pallas_call(
            lambda *refs: kernel(scale_s, *refs),
            out_shape=wide,
            in_specs=[vmem] * len(args),
            out_specs=vmem,
            compiler_params=params(8),
            name=name,
        )(*args)

    grad_image = finish(finish_image_kernel, img_own, img_core, img_home, name="finish_image")
    *txt_home, txt_own, grad_image = lax.optimization_barrier((*txt_home, txt_own, grad_image))
    grad_text = finish(finish_text_kernel, txt_own, *txt_home, name="finish_text")
    return (grad_image, grad_text)


def solution(mesh):
    spec = P(AXES, None)
    return jax.shard_map(
        on_device,
        mesh=mesh,
        in_specs=(spec, spec, spec, spec),
        out_specs=(spec, spec),
        check_vma=False,
    )
```

```python
import math

import jax
import jax.numpy as jnp
from jax import lax
from jax.experimental import pallas as pl
from jax.experimental.pallas import tpu as pltpu
from jax.sharding import PartitionSpec as P

AXES = ("dp", "pair")
MIB = 1024 * 1024
LOG2E = math.log2(math.e)
HEAVY = pl.CostEstimate(flops=10**11, bytes_accessed=10**9, transcendentals=0)
LIGHT = pl.CostEstimate(flops=3 * 10**9, bytes_accessed=3 * 10**7, transcendentals=0)


def send_to(value, place):
    count = lax.axis_size("dp")
    pairs = []
    for block in range(count):
        for member in range(4):
            to_block, to_x, to_core = place(block, member // 2, member % 2)
            pairs.append((block * 4 + member, (to_block % count) * 4 + to_x * 2 + to_core))
    return lax.ppermute(value, AXES, pairs)


def to_other_core(value):
    return send_to(value, lambda block, x, core: (block, x, 1 - core))


def to_other_x(value):
    return send_to(value, lambda block, x, core: (block, 1 - x, core))


def ahead(value, steps):
    return send_to(value, lambda block, x, core: (block + steps, x, core))


def joined(first, second):
    rows = []
    for offset in (0, 2):
        rows += merged(first[offset : offset + 2], second[offset : offset + 2])
    return rows


def pack_kernel(first, second, whole, *parts):
    width = first.shape[1]
    whole[:, :width] = first[...]
    whole[:, width:] = second[...]
    start = 0
    for out in parts:
        here = pl.ds(start, out.shape[0])
        out[:, :width] = first[here]
        out[:, width:] = second[here]
        start += out.shape[0]


def pack_arrived_kernel(s_ahead, t_ahead, s_x, t_x, ahead_out, rest_out, x_out, part_out):
    width, first = s_x.shape[1], part_out.shape[0]
    for student, teacher, whole, part, here in (
        (s_ahead, t_ahead, ahead_out, rest_out, pl.ds(first, s_x.shape[0] - first)),
        (s_x, t_x, x_out, part_out, pl.ds(0, first)),
    ):
        whole[:, :width] = student[...]
        whole[:, width:] = teacher[...]
        part[:, :width] = student[here]
        part[:, width:] = teacher[here]


def rows_of(parts, columns):
    parts = [part[:, columns] for part in parts]
    return parts[0] if len(parts) == 1 else jnp.concatenate(parts, axis=0)


def tile_of(image, texts, span, scale):
    parts = [
        lax.dot_general(
            image,
            rows_of(text, span),
            (((1,), (1,)), ((), ())),
            preferred_element_type=jnp.float32,
        )
        for text in texts
    ]
    tile = parts[0] if len(parts) == 1 else jnp.concatenate(parts, axis=1)
    return tile * (scale * LOG2E)


def stats_along(tile, axis):
    top = jnp.max(tile, axis=axis, keepdims=True)
    below = jnp.exp2(tile - top)
    return top, jnp.sum(below, axis=axis, keepdims=True), below


def merged(first, second):
    top = jnp.maximum(first[0], second[0])
    return top, first[1] * jnp.exp2(first[0] - top) + second[1] * jnp.exp2(second[0] - top)


def as_rows(columns, shard):
    lane = lax.broadcasted_iota(jnp.int32, (shard, 128), 1)
    packed = jnp.zeros((shard, 128), jnp.float32)
    for k, column in enumerate(columns):
        packed = jnp.where(lane == k, column, packed)
    return packed.T[:8]


def score_shards(images, texts, spans, scales, outs, shard):
    stats = [([], []) for _ in images]
    waiting = None
    for step in [(index, which) for index in range(len(images)) for which in range(2)] + [None]:
        tile = None
        if step:
            index, which = step
            image = rows_of(images[index], spans[which])
            tile = tile_of(image, texts, spans[which], scales[which])
        if waiting:
            (index, which), old = waiting
            here = pl.ds(index * shard, shard)
            for axis, found in ((1, stats[index][0]), (0, stats[index][1])):
                top, total, outs[2 * which + 1 - axis][here] = stats_along(old, axis)
                found += (top, total)
        waiting = step, tile
    return stats


def rows4(ref, first, columns=slice(None)):
    part = ref[first : first + 4, columns]
    return [part[k : k + 1] for k in range(4)]


def text_parts(refs, count):
    whole = count - 1
    texts = [(ref,) for ref in refs[:whole]]
    if count == 3:
        return texts + [refs[whole : whole + 1]], refs[whole + 1 :]
    return texts + [refs[whole : whole + 2]], refs[whole + 2 :]


def part_kernel(shard, scales, spans, sizes, count, *refs):
    images = []
    for size in sizes:
        images.append(refs[:size])
        refs = refs[size:]
    texts, refs = text_parts(refs, count)
    outs, (row_out, col_out) = refs[:4], refs[4:]
    stats = score_shards(images, texts, spans, scales, outs, shard)
    for index, (row, column) in enumerate(stats):
        row_out[:, pl.ds(index * shard, shard)] = as_rows(row, shard)
        for k, value in enumerate(column):
            col_out[4 * index + k : 4 * index + k + 1] = value


def far_kernel(shard, scales, spans, *refs):
    outs = refs[13:]
    part_kernel(shard, scales, spans, (2,), 4, *refs[:7], *outs[:6])
    total_kernel(shard, *refs[7:13], outs[4], outs[5], outs[6])


HOME, NEAR, SIDE, FAR = range(4)


def join_calls(rows_in, cols_in, shard):
    rows = []
    for index in range(3):
        call, place = (HOME, index) if index < 2 else (NEAR, 0)
        first = rows4(rows_in[call], 0, pl.ds(place * shard, shard))
        rows.append(joined(first, rows4(rows_in[SIDE], 0, pl.ds(index * shard, shard))))
    rows.append(rows4(rows_in[FAR], 0))
    columns = rows4(cols_in[FAR], 0)
    seen = [part[:, : 3 * shard] for part in columns]
    last = [part[:, 3 * shard :] for part in columns]
    for call, place in ((HOME, 0), (HOME, 1), (NEAR, 0)):
        seen = joined(seen, rows4(cols_in[call], 4 * place))
    for place in range(3):
        last = joined(last, rows4(cols_in[SIDE], 4 * place))
    return rows, seen, last


def total_kernel(shard, *refs):
    rows, seen, last = join_calls(refs[0:8:2], refs[1:8:2], shard)
    out = refs[8]
    for k in range(4):
        for index in range(4):
            out[k : k + 1, index * shard : (index + 1) * shard] = rows[index][k]
        out[4 + k : 5 + k, : 3 * shard] = seen[k]
        out[4 + k : 5 + k, 3 * shard :] = last[k]


def piece_stats(ref, kind, piece, shard):
    part = ref[4 * kind : 4 * kind + 4, piece * shard : (piece + 1) * shard]
    return [part[k : k + 1] for k in range(4)]


def block_parities():
    block = lax.axis_index("dp")
    return lax.rem(block, 2) == 0, lax.rem(block // 2, 2) == 0


def join_group_kernel(shard, mine_ref, core_ref, x_ref, home_ref, *outs):
    halves = []
    for kind, other_ref in enumerate((core_ref, x_ref)):
        for half in range(2):
            joint = []
            for piece in (2 * half, 2 * half + 1):
                total = joined(
                    piece_stats(mine_ref, kind, piece, shard),
                    piece_stats(other_ref, kind, piece ^ 1, shard),
                )
                for k, value in enumerate(total):
                    at = 4 * kind + k
                    home_ref[at : at + 1, piece * shard : (piece + 1) * shard] = value
                joint.append(total)
            halves.append([jnp.concatenate(pair, axis=1) for pair in zip(*joint)])
    for kind, upward in enumerate(block_parities()):
        up, down = halves[2 * kind + kind], halves[2 * kind + 1 - kind]
        for k in range(4):
            outs[2 * kind][k : k + 1] = jnp.where(upward, up[k], down[k])
            outs[2 * kind + 1][k : k + 1] = jnp.where(upward, down[k], up[k])
        for out in outs[2 * kind : 2 * kind + 2]:
            out[4:8] = jnp.zeros((4, 2 * shard), jnp.float32)


def join_blocks_kernel(shard, home_ref, *refs):
    ins, out = refs[:4], refs[4]
    for kind, upward in enumerate(block_parities()):
        first, second = (rows4(ref, 0) for ref in ins[2 * kind : 2 * kind + 2])
        above = [jnp.where(upward, x, y) for x, y in zip(first, second)]
        below = [jnp.where(upward, y, x) for x, y in zip(first, second)]
        for half in range(2):
            here = slice(2 * half * shard, 2 * (half + 1) * shard)
            total = joined(rows4(home_ref, 4 * kind, here), above if half == kind else below)
            for k, value in enumerate(total):
                at = 4 * kind + k
                out[at : at + 1, here] = value


def row_factors(stat_ref, tops, index, shard):
    max_s, total_s, max_t, total_t = rows4(stat_ref, 0, pl.ds(index * shard, shard))
    sub = lax.broadcasted_iota(jnp.int32, (128, shard), 0)
    packed = jnp.zeros((128, shard), jnp.float32)
    for k, (top_s, _, top_t, _) in enumerate(tops):
        packed = jnp.where(sub == 2 * k, jnp.exp2(top_s - max_s) / total_s, packed)
        packed = jnp.where(sub == 2 * k + 1, jnp.exp2(top_t - max_t) / total_t, packed)
    packed = packed.T
    return [packed[:, k : k + 1] for k in range(2 * len(tops))]


def weigh(below, here, columns, row, tops, stats):
    row_s, col_s, row_t, col_t = (ref[here, columns] for ref in below)
    top_s, _, top_t, _ = tops
    max_s, total_s, max_t, total_t = stats
    return (
        row_s * row[0]
        - row_t * row[1]
        + col_s * (jnp.exp2(top_s - max_s) / total_s)
        - col_t * (jnp.exp2(top_t - max_t) / total_t)
    ).astype(jnp.bfloat16)


def text_term(image, weights):
    return lax.dot_general(
        image, weights, (((0,), (0,)), ((), ())), preferred_element_type=jnp.float32
    )


def image_term(weights, texts, span):
    total = None
    for index, text in enumerate(texts):
        shard = weights[0].shape[1] // 2
        part = jnp.dot(
            weights[index // 2][:, (index % 2) * shard : (index % 2 + 1) * shard],
            rows_of(text, span),
            preferred_element_type=jnp.float32,
        )
        total = part if total is None else total + part
    return total


def ahead_kernel(shard, span, *refs):
    below, refs = (refs[0:4], refs[4:8], refs[8:12], refs[12:16]), refs[16:]
    rows_in, cols_in, stat_ref = refs[0:8:2], refs[1:8:2], refs[8]
    images = (refs[9:10], refs[10:11], refs[11:13], refs[13:15])
    texts, refs = text_parts(refs[15:], 4)
    same_out, cross_out, weights_out, img_out, both_out = (
        refs[0:2], refs[2:4], refs[4], refs[5:7], refs[7]
    )
    home, third = slice(0, 2 * shard), slice(2 * shard, 3 * shard)
    fourth, far = slice(3 * shard, 4 * shard), slice(2 * shard, 4 * shard)
    col_home, col_third, col_last, col_far = (
        rows4(stat_ref, 4, at) for at in (home, third, fourth, far)
    )

    def weights_of(index):
        if index == 3:
            here = pl.ds(0, shard)
            row = row_factors(stat_ref, (rows4(rows_in[FAR], 0),), index, shard)
            weights, near = (
                weigh(below[FAR], here, at, row, rows4(cols_in[FAR], 0, at), columns)
                for at, columns in ((far, col_far), (home, col_home))
            )
            return weights, near
        call, place = (HOME, index) if index < 2 else (NEAR, 0)
        here, side = pl.ds(place * shard, shard), pl.ds(index * shard, shard)
        tops = (rows4(rows_in[call], 0, here), rows4(rows_in[SIDE], 0, side))
        row = row_factors(stat_ref, tops, index, shard)
        seen = rows4(cols_in[call], 4 * place, third)
        weights = [weigh(below[call], here, third, row[:2], seen, col_third)]
        seen = rows4(cols_in[SIDE], 4 * index)
        weights.append(weigh(below[SIDE], side, slice(None), row[2:], seen, col_last))
        near = None
        if index == 2:
            seen = rows4(cols_in[call], 4 * place, home)
            near = weigh(below[call], here, home, row[:2], seen, col_home)
        return jnp.concatenate(weights, axis=1), near

    total = both = None
    ready = weights_of(0)
    for index in range(4):
        weights, near = ready
        if index < 3:
            ready = weights_of(index + 1)
        image = rows_of(images[index], span)
        term = text_term(image, weights)
        total = total + term if index else term
        if index < 2:
            weights_out[pl.ds(index * shard, shard)] = weights
            continue
        term = text_term(image, near)
        both = term if index == 2 else both + term
        out = img_out[index - 2]
        out[...] = image_term((near, weights), texts, span).astype(out.dtype)
    height = total.shape[0] // 2
    for index in range(2):
        part = total[index * height : (index + 1) * height]
        same_out[index][...] = part[:, :shard]
        cross_out[index][...] = part[:, shard:].astype(jnp.bfloat16)
    both_out[...] = both


def home_kernel(shard, span, *refs):
    below, (row_in, col_in, stat_ref) = refs[0:4], refs[4:7]
    images = (refs[7:8], refs[8:9])
    texts, (weights_in, both_in, *outs) = text_parts(refs[9:], 4)
    img_out, txt_own, txt_x = outs[0:2], *outs[2:]
    home = slice(0, 2 * shard)
    col_home = rows4(stat_ref, 4, home)
    total = both_in[...]
    for index in range(2):
        here = pl.ds(index * shard, shard)
        row = row_factors(stat_ref, (rows4(row_in, 0, here),), index, shard)
        tops = rows4(col_in, 4 * index, home)
        weights = weigh(below, here, home, row, tops, col_home)
        total = total + text_term(rows_of(images[index], span), weights)
        out = img_out[index]
        out[...] = image_term((weights, weights_in[here]), texts, span).astype(out.dtype)
    txt_own[...] = total[:, :shard]
    txt_x[...] = total[:, shard:].astype(jnp.bfloat16)


def add_kernel(first, second, out):
    total = first[...] + second[...].astype(jnp.float32)
    out[...] = total.astype(out.dtype)


def finish_image_kernel(scale, own, core, home, out):
    total = own[...] + core[...].astype(jnp.float32)
    out[...] = (total + home[...].astype(jnp.float32)) * scale


def finish_text_kernel(scale, own, x, *refs):
    homes, out = refs[:-1], refs[-1]
    width = homes[0].shape[0]
    for index, home in enumerate(homes):
        here = slice(index * width, (index + 1) * width)
        total = own[here] + x[here].astype(jnp.float32) + home[...].astype(jnp.float32)
        out[:, here] = total.T * scale


def on_device(student_image, student_text, teacher_image, teacher_text):
    shard, width_s = student_image.shape
    width_t = teacher_image.shape[1]
    scale_s = 2.0 / math.sqrt(width_s)
    scale_t = 2.0 / math.sqrt(width_t)
    f32 = jnp.float32
    bf16 = jnp.bfloat16
    vmem = pl.BlockSpec(memory_space=pltpu.VMEM)

    def params(mib):
        return pltpu.CompilerParams(vmem_limit_bytes=mib * MIB)


    spans = (slice(0, width_s), slice(width_s, width_s + width_t))
    scales = (scale_s, scale_t)

    def pack(first, second, *heights, name):
        heights = (shard, *heights)
        return pl.pallas_call(
            pack_kernel,
            out_shape=tuple(
                jax.ShapeDtypeStruct((height, width_s + width_t), bf16) for height in heights
            ),
            in_specs=[vmem] * 2,
            out_specs=(vmem,) * len(heights),
            compiler_params=params(8),
            name=name,
        )(first, second)

    text_t_ahead, text_t_x = ahead(teacher_text, -2), to_other_x(teacher_text)
    image_s_core, image_t_core = to_other_core(student_image), to_other_core(teacher_image)
    image, top, bottom = pack(
        student_image, teacher_image, shard * 9 // 16, shard * 7 // 16, name="pack_images"
    )
    bottom = send_to(bottom, lambda block, x, core: (block ^ 1, x, core))
    late_s, image_s_core, image_t_core = lax.optimization_barrier(
        (student_text, image_s_core, image_t_core)
    )
    text_s_ahead, text_s_x = ahead(late_s, -2), to_other_x(late_s)
    top, bottom, late_s, late_t = lax.optimization_barrier(
        (top, bottom, text_s_ahead, text_t_ahead, text_s_x, text_t_x)
    )[:4]
    packed, first = width_s + width_t, shard // 8
    text_ahead, rest, text_x, text_part = pl.pallas_call(
        pack_arrived_kernel,
        out_shape=tuple(
            jax.ShapeDtypeStruct((height, packed), bf16)
            for height in (shard, shard - first, shard, first)
        ),
        in_specs=[vmem] * 4,
        out_specs=(vmem,) * 4,
        compiler_params=params(8),
        name="pack_arrived",
    )(late_s, late_t, text_s_x, text_t_x)
    (text,) = pack(student_text, teacher_text, name="pack_own")
    (image_core,) = pack(image_s_core, image_t_core, name="pack_core")

    def stat(shards):
        return jax.ShapeDtypeStruct((8, shards * shard), f32)

    def score(rows, columns):
        return jax.ShapeDtypeStruct((rows * shard, columns * shard), f32)

    def part_scores(shards, texts, name, cost=None):
        sizes, count = tuple(len(parts) for parts in shards), {3: 3, 2: 1, 5: 4}[len(texts)]
        outs = (score(len(sizes), count),) * 4
        outs += (stat(len(sizes)), jax.ShapeDtypeStruct((4 * len(sizes), count * shard), f32))
        args = [part for parts in shards for part in parts] + list(texts)
        *below, row, col = pl.pallas_call(
            lambda *refs: part_kernel(shard, scales, spans, sizes, count, *refs),
            out_shape=outs,
            in_specs=[vmem] * len(args),
            out_specs=(vmem,) * len(outs),
            compiler_params=params(16),
            cost_estimate=cost,
            name=name,
        )(*args)
        return below, [row, col]

    text_both = (ahead(text_part, -2), to_other_x(rest))
    top = ahead(top, 1)
    bottom = send_to(bottom, lambda block, x, core: (block + 2 - block % 2 * 2, x, core))
    texts = (text, text_x, text_ahead, *text_both)
    own = ((image,), (image_core,))
    home, home_stats = part_scores(own, texts[:3], "scores_home")
    top, bottom = lax.optimization_barrier((top, bottom, home_stats[0]))[:2]
    behind = ((top, bottom), (to_other_core(top), to_other_core(bottom)))
    near, near_stats = part_scores(behind[:1], texts[:3], "scores_near")
    side, side_stats = part_scores((*own, behind[0]), texts[3:], "scores_side", HEAVY)
    others = (*home_stats, *near_stats, *side_stats)
    *far, far_row, far_col, partial = pl.pallas_call(
        lambda *refs: far_kernel(shard, scales, spans, *refs),
        out_shape=(score(1, 4),) * 4
        + (stat(1), jax.ShapeDtypeStruct((4, 4 * shard), f32), stat(4)),
        in_specs=[vmem] * 13,
        out_specs=(vmem,) * 7,
        compiler_params=params(16),
        name="scores_far",
    )(*behind[1], *texts, *others)
    images = (image, image_core, *behind[0], *behind[1])
    calls_stats = (*others, far_row, far_col)

    shared = jax.ShapeDtypeStruct((8, 2 * shard), f32)
    group, *away = pl.pallas_call(
        lambda *refs: join_group_kernel(shard, *refs),
        out_shape=(stat(4),) + (shared,) * 4,
        in_specs=[vmem] * 3,
        out_specs=(vmem,) * 5,
        compiler_params=params(8),
        name="join_group",
    )(partial, to_other_core(partial), to_other_x(partial))
    away = [
        send_to(part, lambda block, x, core, step=step, first=first: (
            block + (step if (block // step) % 2 == first else -step), x, core
        ))
        for part, step, first in zip(away, (1, 1, 2, 2), (0, 1, 0, 1))
    ]
    stats = pl.pallas_call(
        lambda *refs: join_blocks_kernel(shard, *refs),
        out_shape=stat(4),
        in_specs=[vmem] * 5,
        out_specs=vmem,
        compiler_params=params(8),
        name="join_blocks",
    )(group, *away)

    wide = jax.ShapeDtypeStruct((shard, width_s), f32)
    tall = jax.ShapeDtypeStruct((width_s, shard), f32)
    sent = jax.ShapeDtypeStruct((width_s, shard), bf16)
    flat = jax.ShapeDtypeStruct((shard, width_s), bf16)
    tall_half = jax.ShapeDtypeStruct((width_s // 2, shard), f32)
    sent_half = jax.ShapeDtypeStruct((width_s // 2, shard), bf16)
    *txt_ahead, weights, img_back, img_cross, txt_both = pl.pallas_call(
        lambda *refs: ahead_kernel(shard, spans[0], *refs),
        out_shape=(
            tall_half,
            tall_half,
            sent_half,
            sent_half,
            jax.ShapeDtypeStruct((2 * shard, 2 * shard), bf16),
            wide,
            flat,
            jax.ShapeDtypeStruct((width_s, 2 * shard), f32),
        ),
        in_specs=[vmem] * 36,
        out_specs=(vmem,) * 8,
        compiler_params=params(24),
        name="gradients_ahead",
    )(
        *home, *near, *side, *far, *calls_stats, stats,
        *images, *texts,
    )
    img_cross = to_other_core(img_cross)
    img_sum = (img_back + img_cross.astype(f32)).astype(bf16)
    img_home = ahead(img_sum, -1)
    weights = lax.optimization_barrier((weights, img_sum))[0]
    img_own, img_core, txt_own, txt_x = pl.pallas_call(
        lambda *refs: home_kernel(shard, spans[0], *refs),
        out_shape=(wide, flat, tall, sent),
        in_specs=[vmem] * 16,
        out_specs=(vmem,) * 4,
        compiler_params=params(24),
        name="gradients_home",
    )(*home, *home_stats, stats, *images[:2], *texts, weights, txt_both)

    txt_same, txt_cross = txt_ahead[:2], [to_other_x(part) for part in txt_ahead[2:]]
    img_core = to_other_core(img_core)

    def add(first, second, out, name):
        return pl.pallas_call(
            add_kernel,
            out_shape=out,
            in_specs=[vmem] * 2,
            out_specs=vmem,
            compiler_params=params(8),
            cost_estimate=LIGHT,
            name=name,
        )(first, second)

    txt_cross[0] = lax.optimization_barrier((txt_cross[0], img_sum))[0]
    txt_sum = add(txt_same[0], txt_cross[0], sent_half, "add_text")
    txt_x, txt_cross[1] = lax.optimization_barrier((txt_x, txt_cross[1], txt_sum))[:2]
    txt_home = [
        ahead(txt_sum, 2), ahead(add(txt_same[1], txt_cross[1], sent_half, "add_text"), 2)
    ]
    txt_x = to_other_x(txt_x)

    def finish(kernel, *args, name, cost=None):
        return pl.pallas_call(
            lambda *refs: kernel(scale_s, *refs),
            out_shape=wide,
            in_specs=[vmem] * len(args),
            out_specs=vmem,
            compiler_params=params(8),
            cost_estimate=cost,
            name=name,
        )(*args)

    img_home, txt_x = lax.optimization_barrier((img_home, txt_x))
    grad_image = finish(
        finish_image_kernel, img_own, img_core, img_home, name="finish_image", cost=LIGHT
    )
    *txt_home, grad_image = lax.optimization_barrier((*txt_home, grad_image))
    grad_text = finish(finish_text_kernel, txt_own, txt_x, *txt_home, name="finish_text")
    return (grad_image, grad_text)


def solution(mesh):
    spec = P(AXES, None)
    return jax.shard_map(
        on_device,
        mesh=mesh,
        in_specs=(spec, spec, spec, spec),
        out_specs=(spec, spec),
        check_vma=False,
    )
```

```python
import math

import jax
import jax.numpy as jnp
from jax import lax
from jax.experimental import pallas as pl
from jax.experimental.pallas import tpu as pltpu
from jax.sharding import PartitionSpec as P

AXES = ("dp", "pair")
MIB = 1024 * 1024
LOG2E = math.log2(math.e)
HEAVY = pl.CostEstimate(flops=10**11, bytes_accessed=10**9, transcendentals=0)
LIGHT = pl.CostEstimate(flops=3 * 10**9, bytes_accessed=3 * 10**7, transcendentals=0)


def send_to(value, place):
    count = lax.axis_size("dp")
    pairs = []
    for block in range(count):
        for member in range(4):
            to_block, to_x, to_core = place(block, member // 2, member % 2)
            pairs.append((block * 4 + member, (to_block % count) * 4 + to_x * 2 + to_core))
    return lax.ppermute(value, AXES, pairs)


def to_other_core(value):
    return send_to(value, lambda block, x, core: (block, x, 1 - core))


def to_other_x(value):
    return send_to(value, lambda block, x, core: (block, 1 - x, core))


def ahead(value, steps):
    return send_to(value, lambda block, x, core: (block + steps, x, core))


def joined(first, second):
    rows = []
    for offset in (0, 2):
        rows += merged(first[offset : offset + 2], second[offset : offset + 2])
    return rows


def pack_kernel(first, second, whole, *parts):
    width = first.shape[1]
    whole[:, :width] = first[...]
    whole[:, width:] = second[...]
    start = 0
    for out in parts:
        here = pl.ds(start, out.shape[0])
        out[:, :width] = first[here]
        out[:, width:] = second[here]
        start += out.shape[0]


def pack_arrived_kernel(s_ahead, t_ahead, s_x, t_x, ahead_out, rest_out, x_out, part_out):
    width, first = s_x.shape[1], part_out.shape[0]
    for student, teacher, whole, part, here in (
        (s_ahead, t_ahead, ahead_out, rest_out, pl.ds(first, s_x.shape[0] - first)),
        (s_x, t_x, x_out, part_out, pl.ds(0, first)),
    ):
        whole[:, :width] = student[...]
        whole[:, width:] = teacher[...]
        part[:, :width] = student[here]
        part[:, width:] = teacher[here]


def rows_of(parts, columns):
    parts = [part[:, columns] for part in parts]
    return parts[0] if len(parts) == 1 else jnp.concatenate(parts, axis=0)


def tile_of(image, texts, span, scale):
    parts = [
        lax.dot_general(
            image,
            rows_of(text, span),
            (((1,), (1,)), ((), ())),
            preferred_element_type=jnp.float32,
        )
        for text in texts
    ]
    tile = parts[0] if len(parts) == 1 else jnp.concatenate(parts, axis=1)
    return tile * (scale * LOG2E)


def stats_along(tile, axis):
    top = jnp.max(tile, axis=axis, keepdims=True)
    below = jnp.exp2(tile - top)
    return top, jnp.sum(below, axis=axis, keepdims=True), below


def merged(first, second):
    top = jnp.maximum(first[0], second[0])
    return top, first[1] * jnp.exp2(first[0] - top) + second[1] * jnp.exp2(second[0] - top)


def as_rows(columns, shard):
    lane = lax.broadcasted_iota(jnp.int32, (shard, 128), 1)
    packed = jnp.zeros((shard, 128), jnp.float32)
    for k, column in enumerate(columns):
        packed = jnp.where(lane == k, column, packed)
    return packed.T[:8]


def score_shards(images, texts, spans, scales, outs, shard):
    stats = [([], []) for _ in images]
    waiting = None
    for step in [(index, which) for index in range(len(images)) for which in range(2)] + [None]:
        tile = None
        if step:
            index, which = step
            image = rows_of(images[index], spans[which])
            tile = tile_of(image, texts, spans[which], scales[which])
        if waiting:
            (index, which), old = waiting
            here = pl.ds(index * shard, shard)
            for axis, found in ((1, stats[index][0]), (0, stats[index][1])):
                top, total, outs[2 * which + 1 - axis][here] = stats_along(old, axis)
                found += (top, total)
        waiting = step, tile
    return stats


def rows4(ref, first, columns=slice(None)):
    part = ref[first : first + 4, columns]
    return [part[k : k + 1] for k in range(4)]


def text_parts(refs, count):
    whole = count - 1
    texts = [(ref,) for ref in refs[:whole]]
    if count == 3:
        return texts + [refs[whole : whole + 1]], refs[whole + 1 :]
    return texts + [refs[whole : whole + 2]], refs[whole + 2 :]


def part_kernel(shard, scales, spans, sizes, count, *refs):
    images = []
    for size in sizes:
        images.append(refs[:size])
        refs = refs[size:]
    texts, refs = text_parts(refs, count)
    outs, (row_out, col_out) = refs[:4], refs[4:]
    stats = score_shards(images, texts, spans, scales, outs, shard)
    for index, (row, column) in enumerate(stats):
        row_out[:, pl.ds(index * shard, shard)] = as_rows(row, shard)
        for k, value in enumerate(column):
            col_out[4 * index + k : 4 * index + k + 1] = value


def far_kernel(shard, scales, spans, *refs):
    outs = refs[13:]
    part_kernel(shard, scales, spans, (2,), 4, *refs[:7], *outs[:6])
    total_kernel(shard, *refs[7:13], outs[4], outs[5], outs[6])


HOME, NEAR, SIDE, FAR = range(4)


def join_calls(rows_in, cols_in, shard):
    rows = []
    for index in range(3):
        call, place = (HOME, index) if index < 2 else (NEAR, 0)
        first = rows4(rows_in[call], 0, pl.ds(place * shard, shard))
        rows.append(joined(first, rows4(rows_in[SIDE], 0, pl.ds(index * shard, shard))))
    rows.append(rows4(rows_in[FAR], 0))
    columns = rows4(cols_in[FAR], 0)
    seen = [part[:, : 3 * shard] for part in columns]
    last = [part[:, 3 * shard :] for part in columns]
    for call, place in ((HOME, 0), (HOME, 1), (NEAR, 0)):
        seen = joined(seen, rows4(cols_in[call], 4 * place))
    for place in range(3):
        last = joined(last, rows4(cols_in[SIDE], 4 * place))
    return rows, seen, last


def total_kernel(shard, *refs):
    rows, seen, last = join_calls(refs[0:8:2], refs[1:8:2], shard)
    out = refs[8]
    for k in range(4):
        for index in range(4):
            out[k : k + 1, index * shard : (index + 1) * shard] = rows[index][k]
        out[4 + k : 5 + k, : 3 * shard] = seen[k]
        out[4 + k : 5 + k, 3 * shard :] = last[k]


def piece_stats(ref, kind, piece, shard):
    part = ref[4 * kind : 4 * kind + 4, piece * shard : (piece + 1) * shard]
    return [part[k : k + 1] for k in range(4)]


def block_parities():
    block = lax.axis_index("dp")
    return lax.rem(block, 2) == 0, lax.rem(block // 2, 2) == 0


def join_group_kernel(shard, mine_ref, core_ref, x_ref, home_ref, *outs):
    halves = []
    for kind, other_ref in enumerate((core_ref, x_ref)):
        for half in range(2):
            joint = []
            for piece in (2 * half, 2 * half + 1):
                total = joined(
                    piece_stats(mine_ref, kind, piece, shard),
                    piece_stats(other_ref, kind, piece ^ 1, shard),
                )
                for k, value in enumerate(total):
                    at = 4 * kind + k
                    home_ref[at : at + 1, piece * shard : (piece + 1) * shard] = value
                joint.append(total)
            halves.append([jnp.concatenate(pair, axis=1) for pair in zip(*joint)])
    for kind, upward in enumerate(block_parities()):
        up, down = halves[2 * kind + kind], halves[2 * kind + 1 - kind]
        for k in range(4):
            outs[2 * kind][k : k + 1] = jnp.where(upward, up[k], down[k])
            outs[2 * kind + 1][k : k + 1] = jnp.where(upward, down[k], up[k])
        for out in outs[2 * kind : 2 * kind + 2]:
            out[4:8] = jnp.zeros((4, 2 * shard), jnp.float32)


def join_blocks_kernel(shard, home_ref, *refs):
    ins, out = refs[:4], refs[4]
    for kind, upward in enumerate(block_parities()):
        first, second = (rows4(ref, 0) for ref in ins[kind::2])
        above = [jnp.where(upward, x, y) for x, y in zip(first, second)]
        below = [jnp.where(upward, y, x) for x, y in zip(first, second)]
        for half in range(2):
            here = slice(2 * half * shard, 2 * (half + 1) * shard)
            total = joined(rows4(home_ref, 4 * kind, here), above if half == kind else below)
            for k, value in enumerate(total):
                at = 4 * kind + k
                out[at : at + 1, here] = value


def row_factors(stat_ref, tops, index, shard):
    max_s, total_s, max_t, total_t = rows4(stat_ref, 0, pl.ds(index * shard, shard))
    sub = lax.broadcasted_iota(jnp.int32, (128, shard), 0)
    packed = jnp.zeros((128, shard), jnp.float32)
    for k, (top_s, _, top_t, _) in enumerate(tops):
        packed = jnp.where(sub == 2 * k, jnp.exp2(top_s - max_s) / total_s, packed)
        packed = jnp.where(sub == 2 * k + 1, jnp.exp2(top_t - max_t) / total_t, packed)
    packed = packed.T
    return [packed[:, k : k + 1] for k in range(2 * len(tops))]


def weigh(below, here, columns, row, tops, stats):
    row_s, col_s, row_t, col_t = (ref[here, columns] for ref in below)
    top_s, _, top_t, _ = tops
    max_s, total_s, max_t, total_t = stats
    return (
        row_s * row[0]
        - row_t * row[1]
        + col_s * (jnp.exp2(top_s - max_s) / total_s)
        - col_t * (jnp.exp2(top_t - max_t) / total_t)
    ).astype(jnp.bfloat16)


def text_term(image, weights):
    return lax.dot_general(
        image, weights, (((0,), (0,)), ((), ())), preferred_element_type=jnp.float32
    )


def image_term(weights, texts, span):
    total = None
    for index, text in enumerate(texts):
        shard = weights[0].shape[1] // 2
        part = jnp.dot(
            weights[index // 2][:, (index % 2) * shard : (index % 2 + 1) * shard],
            rows_of(text, span),
            preferred_element_type=jnp.float32,
        )
        total = part if total is None else total + part
    return total


def ahead_kernel(shard, span, *refs):
    below, refs = (refs[0:4], refs[4:8], refs[8:12], refs[12:16]), refs[16:]
    rows_in, cols_in, stat_ref = refs[0:8:2], refs[1:8:2], refs[8]
    images = (refs[9:10], refs[10:11], refs[11:13], refs[13:15])
    texts, refs = text_parts(refs[15:], 4)
    same_out, cross_out, weights_out, img_out, both_out = (
        refs[0:2], refs[2:4], refs[4], refs[5:7], refs[7]
    )
    home, third = slice(0, 2 * shard), slice(2 * shard, 3 * shard)
    fourth, far = slice(3 * shard, 4 * shard), slice(2 * shard, 4 * shard)
    col_home, col_third, col_last, col_far = (
        rows4(stat_ref, 4, at) for at in (home, third, fourth, far)
    )

    def weights_of(index):
        if index == 3:
            here = pl.ds(0, shard)
            row = row_factors(stat_ref, (rows4(rows_in[FAR], 0),), index, shard)
            weights, near = (
                weigh(below[FAR], here, at, row, rows4(cols_in[FAR], 0, at), columns)
                for at, columns in ((far, col_far), (home, col_home))
            )
            return weights, near
        call, place = (HOME, index) if index < 2 else (NEAR, 0)
        here, side = pl.ds(place * shard, shard), pl.ds(index * shard, shard)
        tops = (rows4(rows_in[call], 0, here), rows4(rows_in[SIDE], 0, side))
        row = row_factors(stat_ref, tops, index, shard)
        seen = rows4(cols_in[call], 4 * place, third)
        weights = [weigh(below[call], here, third, row[:2], seen, col_third)]
        seen = rows4(cols_in[SIDE], 4 * index)
        weights.append(weigh(below[SIDE], side, slice(None), row[2:], seen, col_last))
        near = None
        if index == 2:
            seen = rows4(cols_in[call], 4 * place, home)
            near = weigh(below[call], here, home, row[:2], seen, col_home)
        return jnp.concatenate(weights, axis=1), near

    total = both = None
    ready = weights_of(0)
    for index in range(4):
        weights, near = ready
        if index < 3:
            ready = weights_of(index + 1)
        image = rows_of(images[index], span)
        term = text_term(image, weights)
        total = total + term if index else term
        if index < 2:
            weights_out[pl.ds(index * shard, shard)] = weights
            continue
        term = text_term(image, near)
        both = term if index == 2 else both + term
        out = img_out[index - 2]
        out[...] = image_term((near, weights), texts, span).astype(out.dtype)
    height = total.shape[0] // 2
    for index in range(2):
        part = total[index * height : (index + 1) * height]
        same_out[index][...] = part[:, :shard]
        cross_out[index][...] = part[:, shard:].astype(jnp.bfloat16)
    both_out[...] = both


def home_kernel(shard, span, *refs):
    below, (row_in, col_in, stat_ref) = refs[0:4], refs[4:7]
    images = (refs[7:8], refs[8:9])
    texts, (weights_in, both_in, *outs) = text_parts(refs[9:], 4)
    img_out, txt_own, txt_x = outs[0:2], *outs[2:]
    home = slice(0, 2 * shard)
    col_home = rows4(stat_ref, 4, home)
    total = both_in[...]
    for index in range(2):
        here = pl.ds(index * shard, shard)
        row = row_factors(stat_ref, (rows4(row_in, 0, here),), index, shard)
        tops = rows4(col_in, 4 * index, home)
        weights = weigh(below, here, home, row, tops, col_home)
        total = total + text_term(rows_of(images[index], span), weights)
        out = img_out[index]
        out[...] = image_term((weights, weights_in[here]), texts, span).astype(out.dtype)
    txt_own[...] = total[:, :shard]
    txt_x[...] = total[:, shard:].astype(jnp.bfloat16)


def add_kernel(first, second, out):
    total = first[...] + second[...].astype(jnp.float32)
    out[...] = total.astype(out.dtype)


def finish_image_kernel(scale, own, core, home, out):
    total = own[...] + core[...].astype(jnp.float32)
    out[...] = (total + home[...].astype(jnp.float32)) * scale


def finish_text_kernel(scale, own, x, *refs):
    homes, out = refs[:-1], refs[-1]
    width = homes[0].shape[0]
    for index, home in enumerate(homes):
        here = slice(index * width, (index + 1) * width)
        total = own[here] + x[here].astype(jnp.float32) + home[...].astype(jnp.float32)
        out[:, here] = total.T * scale


def on_device(student_image, student_text, teacher_image, teacher_text):
    shard, width_s = student_image.shape
    width_t = teacher_image.shape[1]
    scale_s = 2.0 / math.sqrt(width_s)
    scale_t = 2.0 / math.sqrt(width_t)
    f32 = jnp.float32
    bf16 = jnp.bfloat16
    vmem = pl.BlockSpec(memory_space=pltpu.VMEM)

    def params(mib):
        return pltpu.CompilerParams(vmem_limit_bytes=mib * MIB)


    spans = (slice(0, width_s), slice(width_s, width_s + width_t))
    scales = (scale_s, scale_t)

    def pack(first, second, *heights, name):
        heights = (shard, *heights)
        return pl.pallas_call(
            pack_kernel,
            out_shape=tuple(
                jax.ShapeDtypeStruct((height, width_s + width_t), bf16) for height in heights
            ),
            in_specs=[vmem] * 2,
            out_specs=(vmem,) * len(heights),
            compiler_params=params(8),
            name=name,
        )(first, second)

    text_t_ahead, text_t_x = ahead(teacher_text, -2), to_other_x(teacher_text)
    image_s_core, image_t_core = to_other_core(student_image), to_other_core(teacher_image)
    image, top, bottom = pack(
        student_image, teacher_image, shard * 9 // 16, shard * 7 // 16, name="pack_images"
    )
    bottom = send_to(bottom, lambda block, x, core: (block ^ 1, x, core))
    late_s, image_s_core, image_t_core = lax.optimization_barrier(
        (student_text, image_s_core, image_t_core)
    )
    text_s_ahead, text_s_x = ahead(late_s, -2), to_other_x(late_s)
    top, bottom, late_s, late_t = lax.optimization_barrier(
        (top, bottom, text_s_ahead, text_t_ahead, text_s_x, text_t_x)
    )[:4]
    packed, first = width_s + width_t, shard // 8
    text_ahead, rest, text_x, text_part = pl.pallas_call(
        pack_arrived_kernel,
        out_shape=tuple(
            jax.ShapeDtypeStruct((height, packed), bf16)
            for height in (shard, shard - first, shard, first)
        ),
        in_specs=[vmem] * 4,
        out_specs=(vmem,) * 4,
        compiler_params=params(8),
        name="pack_arrived",
    )(late_s, late_t, text_s_x, text_t_x)
    (text,) = pack(student_text, teacher_text, name="pack_own")
    (image_core,) = pack(image_s_core, image_t_core, name="pack_core")

    def stat(shards):
        return jax.ShapeDtypeStruct((8, shards * shard), f32)

    def score(rows, columns):
        return jax.ShapeDtypeStruct((rows * shard, columns * shard), f32)

    def part_scores(shards, texts, name, cost=None):
        sizes, count = tuple(len(parts) for parts in shards), {3: 3, 2: 1, 5: 4}[len(texts)]
        outs = (score(len(sizes), count),) * 4
        outs += (stat(len(sizes)), jax.ShapeDtypeStruct((4 * len(sizes), count * shard), f32))
        args = [part for parts in shards for part in parts] + list(texts)
        *below, row, col = pl.pallas_call(
            lambda *refs: part_kernel(shard, scales, spans, sizes, count, *refs),
            out_shape=outs,
            in_specs=[vmem] * len(args),
            out_specs=(vmem,) * len(outs),
            compiler_params=params(16),
            cost_estimate=cost,
            name=name,
        )(*args)
        return below, [row, col]

    text_both = (ahead(text_part, -2), to_other_x(rest))
    top = ahead(top, 1)
    bottom = send_to(bottom, lambda block, x, core: (block + 2 - block % 2 * 2, x, core))
    texts = (text, text_x, text_ahead, *text_both)
    own = ((image,), (image_core,))
    home, home_stats = part_scores(own, texts[:3], "scores_home")
    top, bottom = lax.optimization_barrier((top, bottom, home_stats[0]))[:2]
    behind = ((top, bottom), (to_other_core(top), to_other_core(bottom)))
    near, near_stats = part_scores(behind[:1], texts[:3], "scores_near")
    side, side_stats = part_scores((*own, behind[0]), texts[3:], "scores_side", HEAVY)
    others = (*home_stats, *near_stats, *side_stats)
    *far, far_row, far_col, partial = pl.pallas_call(
        lambda *refs: far_kernel(shard, scales, spans, *refs),
        out_shape=(score(1, 4),) * 4
        + (stat(1), jax.ShapeDtypeStruct((4, 4 * shard), f32), stat(4)),
        in_specs=[vmem] * 13,
        out_specs=(vmem,) * 7,
        compiler_params=params(16),
        name="scores_far",
    )(*behind[1], *texts, *others)
    images = (image, image_core, *behind[0], *behind[1])
    calls_stats = (*others, far_row, far_col)

    shared = jax.ShapeDtypeStruct((8, 2 * shard), f32)
    group, *away = pl.pallas_call(
        lambda *refs: join_group_kernel(shard, *refs),
        out_shape=(stat(4),) + (shared,) * 4,
        in_specs=[vmem] * 3,
        out_specs=(vmem,) * 5,
        compiler_params=params(8),
        name="join_group",
    )(partial, to_other_core(partial), to_other_x(partial))
    away = [
        send_to(away[index], lambda block, x, core, step=step, first=first: (
            block + (step if (block // step) % 2 == first else -step), x, core
        ))
        for index, step, first in ((0, 1, 0), (2, 2, 0), (1, 1, 1), (3, 2, 1))
    ]
    stats = pl.pallas_call(
        lambda *refs: join_blocks_kernel(shard, *refs),
        out_shape=stat(4),
        in_specs=[vmem] * 5,
        out_specs=vmem,
        compiler_params=params(8),
        name="join_blocks",
    )(group, *away)

    wide = jax.ShapeDtypeStruct((shard, width_s), f32)
    tall = jax.ShapeDtypeStruct((width_s, shard), f32)
    sent = jax.ShapeDtypeStruct((width_s, shard), bf16)
    flat = jax.ShapeDtypeStruct((shard, width_s), bf16)
    tall_half = jax.ShapeDtypeStruct((width_s // 2, shard), f32)
    sent_half = jax.ShapeDtypeStruct((width_s // 2, shard), bf16)
    *txt_ahead, weights, img_back, img_cross, txt_both = pl.pallas_call(
        lambda *refs: ahead_kernel(shard, spans[0], *refs),
        out_shape=(
            tall_half,
            tall_half,
            sent_half,
            sent_half,
            jax.ShapeDtypeStruct((2 * shard, 2 * shard), bf16),
            wide,
            flat,
            jax.ShapeDtypeStruct((width_s, 2 * shard), f32),
        ),
        in_specs=[vmem] * 36,
        out_specs=(vmem,) * 8,
        compiler_params=params(24),
        name="gradients_ahead",
    )(
        *home, *near, *side, *far, *calls_stats, stats,
        *images, *texts,
    )
    img_cross = to_other_core(img_cross)
    img_sum = (img_back + img_cross.astype(f32)).astype(bf16)
    img_home = ahead(img_sum, -1)
    weights = lax.optimization_barrier((weights, img_sum))[0]
    img_own, img_core, txt_own, txt_x = pl.pallas_call(
        lambda *refs: home_kernel(shard, spans[0], *refs),
        out_shape=(wide, flat, tall, sent),
        in_specs=[vmem] * 16,
        out_specs=(vmem,) * 4,
        compiler_params=params(24),
        name="gradients_home",
    )(*home, *home_stats, stats, *images[:2], *texts, weights, txt_both)

    txt_same, txt_cross = txt_ahead[:2], [to_other_x(part) for part in txt_ahead[2:]]
    img_core = to_other_core(img_core)

    def add(first, second, out, name):
        return pl.pallas_call(
            add_kernel,
            out_shape=out,
            in_specs=[vmem] * 2,
            out_specs=vmem,
            compiler_params=params(8),
            cost_estimate=LIGHT,
            name=name,
        )(first, second)

    txt_cross[0] = lax.optimization_barrier((txt_cross[0], img_sum))[0]
    txt_sum = add(txt_same[0], txt_cross[0], sent_half, "add_text")
    txt_x, txt_cross[1] = lax.optimization_barrier((txt_x, txt_cross[1], txt_sum))[:2]
    txt_home = [
        ahead(txt_sum, 2), ahead(add(txt_same[1], txt_cross[1], sent_half, "add_text"), 2)
    ]
    txt_x = to_other_x(txt_x)

    def finish(kernel, *args, name, cost=None):
        return pl.pallas_call(
            lambda *refs: kernel(scale_s, *refs),
            out_shape=wide,
            in_specs=[vmem] * len(args),
            out_specs=vmem,
            compiler_params=params(8),
            cost_estimate=cost,
            name=name,
        )(*args)

    img_home, txt_x = lax.optimization_barrier((img_home, txt_x))
    grad_image = finish(
        finish_image_kernel, img_own, img_core, img_home, name="finish_image", cost=LIGHT
    )
    *txt_home, grad_image = lax.optimization_barrier((*txt_home, grad_image))
    grad_text = finish(finish_text_kernel, txt_own, txt_x, *txt_home, name="finish_text")
    return (grad_image, grad_text)


def solution(mesh):
    spec = P(AXES, None)
    return jax.shard_map(
        on_device,
        mesh=mesh,
        in_specs=(spec, spec, spec, spec),
        out_specs=(spec, spec),
        check_vma=False,
    )
```

```python
import math

import jax
import jax.numpy as jnp
from jax import lax
from jax.experimental import pallas as pl
from jax.experimental.pallas import tpu as pltpu
from jax.sharding import PartitionSpec as P

AXES = ("dp", "pair")
MIB = 1024 * 1024
LOG2E = math.log2(math.e)
HEAVY = pl.CostEstimate(flops=10**11, bytes_accessed=10**9, transcendentals=0)
LIGHT = pl.CostEstimate(flops=3 * 10**9, bytes_accessed=3 * 10**7, transcendentals=0)


def send_to(value, place):
    count = lax.axis_size("dp")
    pairs = []
    for block in range(count):
        for member in range(4):
            to_block, to_x, to_core = place(block, member // 2, member % 2)
            pairs.append((block * 4 + member, (to_block % count) * 4 + to_x * 2 + to_core))
    return lax.ppermute(value, AXES, pairs)


def to_other_core(value):
    return send_to(value, lambda block, x, core: (block, x, 1 - core))


def to_other_x(value):
    return send_to(value, lambda block, x, core: (block, 1 - x, core))


def ahead(value, steps):
    return send_to(value, lambda block, x, core: (block + steps, x, core))


def joined(first, second):
    rows = []
    for offset in (0, 2):
        rows += merged(first[offset : offset + 2], second[offset : offset + 2])
    return rows


def pack_kernel(first, second, whole, *parts):
    width = first.shape[1]
    whole[:, :width] = first[...]
    whole[:, width:] = second[...]
    start = 0
    for out in parts:
        here = pl.ds(start, out.shape[0])
        out[:, :width] = first[here]
        out[:, width:] = second[here]
        start += out.shape[0]


def pack_arrived_kernel(s_ahead, t_ahead, s_x, t_x, ahead_out, rest_out, x_out, part_out):
    width, first = s_x.shape[1], part_out.shape[0]
    for student, teacher, whole, part, here in (
        (s_ahead, t_ahead, ahead_out, rest_out, pl.ds(first, s_x.shape[0] - first)),
        (s_x, t_x, x_out, part_out, pl.ds(0, first)),
    ):
        whole[:, :width] = student[...]
        whole[:, width:] = teacher[...]
        part[:, :width] = student[here]
        part[:, width:] = teacher[here]


def rows_of(parts, columns):
    parts = [part[:, columns] for part in parts]
    return parts[0] if len(parts) == 1 else jnp.concatenate(parts, axis=0)


def tile_of(image, texts, span, scale):
    parts = [
        lax.dot_general(
            image,
            rows_of(text, span),
            (((1,), (1,)), ((), ())),
            preferred_element_type=jnp.float32,
        )
        for text in texts
    ]
    tile = parts[0] if len(parts) == 1 else jnp.concatenate(parts, axis=1)
    return tile * (scale * LOG2E)


def stats_along(tile, axis):
    top = jnp.max(tile, axis=axis, keepdims=True)
    below = jnp.exp2(tile - top)
    return top, jnp.sum(below, axis=axis, keepdims=True), below


def merged(first, second):
    top = jnp.maximum(first[0], second[0])
    return top, first[1] * jnp.exp2(first[0] - top) + second[1] * jnp.exp2(second[0] - top)


def as_rows(columns, shard):
    lane = lax.broadcasted_iota(jnp.int32, (shard, 128), 1)
    packed = jnp.zeros((shard, 128), jnp.float32)
    for k, column in enumerate(columns):
        packed = jnp.where(lane == k, column, packed)
    return packed.T[:8]


def score_shards(images, texts, spans, scales, outs, shard):
    stats = [([], []) for _ in images]
    waiting = None
    for step in [(index, which) for index in range(len(images)) for which in range(2)] + [None]:
        tile = None
        if step:
            index, which = step
            image = rows_of(images[index], spans[which])
            tile = tile_of(image, texts, spans[which], scales[which])
        if waiting:
            (index, which), old = waiting
            here = pl.ds(index * shard, shard)
            for axis, found in ((1, stats[index][0]), (0, stats[index][1])):
                top, total, outs[2 * which + 1 - axis][here] = stats_along(old, axis)
                found += (top, total)
        waiting = step, tile
    return stats


def rows4(ref, first, columns=slice(None)):
    part = ref[first : first + 4, columns]
    return [part[k : k + 1] for k in range(4)]


def text_parts(refs, count):
    whole = count - 1
    texts = [(ref,) for ref in refs[:whole]]
    if count == 3:
        return texts + [refs[whole : whole + 1]], refs[whole + 1 :]
    return texts + [refs[whole : whole + 2]], refs[whole + 2 :]


def part_kernel(shard, scales, spans, sizes, count, *refs):
    images = []
    for size in sizes:
        images.append(refs[:size])
        refs = refs[size:]
    texts, refs = text_parts(refs, count)
    outs, (row_out, col_out) = refs[:4], refs[4:]
    stats = score_shards(images, texts, spans, scales, outs, shard)
    for index, (row, column) in enumerate(stats):
        row_out[:, pl.ds(index * shard, shard)] = as_rows(row, shard)
        for k, value in enumerate(column):
            col_out[4 * index + k : 4 * index + k + 1] = value


def far_kernel(shard, scales, spans, *refs):
    outs = refs[13:]
    part_kernel(shard, scales, spans, (2,), 4, *refs[:7], *outs[:6])
    total_kernel(shard, *refs[7:13], outs[4], outs[5], outs[6])


HOME, NEAR, SIDE, FAR = range(4)


def join_calls(rows_in, cols_in, shard):
    rows = []
    for index in range(3):
        call, place = (HOME, index) if index < 2 else (NEAR, 0)
        first = rows4(rows_in[call], 0, pl.ds(place * shard, shard))
        rows.append(joined(first, rows4(rows_in[SIDE], 0, pl.ds(index * shard, shard))))
    rows.append(rows4(rows_in[FAR], 0))
    columns = rows4(cols_in[FAR], 0)
    seen = [part[:, : 3 * shard] for part in columns]
    last = [part[:, 3 * shard :] for part in columns]
    for call, place in ((HOME, 0), (HOME, 1), (NEAR, 0)):
        seen = joined(seen, rows4(cols_in[call], 4 * place))
    for place in range(3):
        last = joined(last, rows4(cols_in[SIDE], 4 * place))
    return rows, seen, last


def total_kernel(shard, *refs):
    rows, seen, last = join_calls(refs[0:8:2], refs[1:8:2], shard)
    out = refs[8]
    for k in range(4):
        for index in range(4):
            out[k : k + 1, index * shard : (index + 1) * shard] = rows[index][k]
        out[4 + k : 5 + k, : 3 * shard] = seen[k]
        out[4 + k : 5 + k, 3 * shard :] = last[k]


def piece_stats(ref, kind, piece, shard):
    part = ref[4 * kind : 4 * kind + 4, piece * shard : (piece + 1) * shard]
    return [part[k : k + 1] for k in range(4)]


def block_parities():
    block = lax.axis_index("dp")
    return lax.rem(block, 2) == 0, lax.rem(block // 2, 2) == 0


def join_group_kernel(shard, mine_ref, core_ref, x_ref, home_ref, *outs):
    halves = []
    for kind, other_ref in enumerate((core_ref, x_ref)):
        for half in range(2):
            joint = []
            for piece in (2 * half, 2 * half + 1):
                total = joined(
                    piece_stats(mine_ref, kind, piece, shard),
                    piece_stats(other_ref, kind, piece ^ 1, shard),
                )
                for k, value in enumerate(total):
                    at = 4 * kind + k
                    home_ref[at : at + 1, piece * shard : (piece + 1) * shard] = value
                joint.append(total)
            halves.append([jnp.concatenate(pair, axis=1) for pair in zip(*joint)])
    for kind, upward in enumerate(block_parities()):
        up, down = halves[2 * kind + kind], halves[2 * kind + 1 - kind]
        for k in range(4):
            outs[2 * kind][k : k + 1] = jnp.where(upward, up[k], down[k])
            outs[2 * kind + 1][k : k + 1] = jnp.where(upward, down[k], up[k])
        for out in outs[2 * kind : 2 * kind + 2]:
            out[4:8] = jnp.zeros((4, 2 * shard), jnp.float32)


def join_blocks_kernel(shard, home_ref, *refs):
    ins, out = refs[:4], refs[4]
    for kind, upward in enumerate(block_parities()):
        first, second = (rows4(ref, 0) for ref in ins[kind::2])
        above = [jnp.where(upward, x, y) for x, y in zip(first, second)]
        below = [jnp.where(upward, y, x) for x, y in zip(first, second)]
        for half in range(2):
            here = slice(2 * half * shard, 2 * (half + 1) * shard)
            total = joined(rows4(home_ref, 4 * kind, here), above if half == kind else below)
            for k, value in enumerate(total):
                at = 4 * kind + k
                out[at : at + 1, here] = value


def row_factors(stat_ref, tops, index, shard):
    max_s, total_s, max_t, total_t = rows4(stat_ref, 0, pl.ds(index * shard, shard))
    sub = lax.broadcasted_iota(jnp.int32, (128, shard), 0)
    packed = jnp.zeros((128, shard), jnp.float32)
    for k, (top_s, _, top_t, _) in enumerate(tops):
        packed = jnp.where(sub == 2 * k, jnp.exp2(top_s - max_s) / total_s, packed)
        packed = jnp.where(sub == 2 * k + 1, jnp.exp2(top_t - max_t) / total_t, packed)
    packed = packed.T
    return [packed[:, k : k + 1] for k in range(2 * len(tops))]


def weigh(below, here, columns, row, tops, stats):
    row_s, col_s, row_t, col_t = (ref[here, columns] for ref in below)
    top_s, _, top_t, _ = tops
    max_s, total_s, max_t, total_t = stats
    return (
        row_s * row[0]
        - row_t * row[1]
        + col_s * (jnp.exp2(top_s - max_s) / total_s)
        - col_t * (jnp.exp2(top_t - max_t) / total_t)
    ).astype(jnp.bfloat16)


def text_term(image, weights):
    return lax.dot_general(
        image, weights, (((0,), (0,)), ((), ())), preferred_element_type=jnp.float32
    )


def image_term(weights, texts, span):
    total = None
    for index, text in enumerate(texts):
        shard = weights[0].shape[1] // 2
        part = jnp.dot(
            weights[index // 2][:, (index % 2) * shard : (index % 2 + 1) * shard],
            rows_of(text, span),
            preferred_element_type=jnp.float32,
        )
        total = part if total is None else total + part
    return total


def ahead_kernel(shard, span, behind, *refs):
    below, refs = (refs[0:4], refs[4:8], refs[8:12], refs[12:16]), refs[16:]
    rows_in, cols_in, stat_ref = refs[0:8:2], refs[1:8:2], refs[8]
    images = (refs[9:10], refs[10:11], refs[11:13], refs[13:15])
    texts, refs = text_parts(refs[15:], 4)
    if behind:
        total_out, img_out, both_out = refs[0], refs[1:3], refs[3]
    else:
        total_in, same_out, cross_out, weights_out = refs[0], refs[1:3], refs[3:5], refs[5]
    home, third = slice(0, 2 * shard), slice(2 * shard, 3 * shard)
    fourth, far = slice(3 * shard, 4 * shard), slice(2 * shard, 4 * shard)
    col_home, col_third, col_last, col_far = (
        rows4(stat_ref, 4, at) for at in (home, third, fourth, far)
    )

    def weights_of(index):
        if index == 3:
            here = pl.ds(0, shard)
            row = row_factors(stat_ref, (rows4(rows_in[FAR], 0),), index, shard)
            weights, near = (
                weigh(below[FAR], here, at, row, rows4(cols_in[FAR], 0, at), columns)
                for at, columns in ((far, col_far), (home, col_home))
            )
            return weights, near
        call, place = (HOME, index) if index < 2 else (NEAR, 0)
        here, side = pl.ds(place * shard, shard), pl.ds(index * shard, shard)
        tops = (rows4(rows_in[call], 0, here), rows4(rows_in[SIDE], 0, side))
        row = row_factors(stat_ref, tops, index, shard)
        seen = rows4(cols_in[call], 4 * place, third)
        weights = [weigh(below[call], here, third, row[:2], seen, col_third)]
        seen = rows4(cols_in[SIDE], 4 * index)
        weights.append(weigh(below[SIDE], side, slice(None), row[2:], seen, col_last))
        near = None
        if index == 2:
            seen = rows4(cols_in[call], 4 * place, home)
            near = weigh(below[call], here, home, row[:2], seen, col_home)
        return jnp.concatenate(weights, axis=1), near

    both = None
    total = None if behind else total_in[...]
    for index in (2, 3) if behind else (0, 1):
        weights, near = weights_of(index)
        image = rows_of(images[index], span)
        term = text_term(image, weights)
        total = term if total is None else total + term
        if index < 2:
            weights_out[pl.ds(index * shard, shard)] = weights
            continue
        term = text_term(image, near)
        both = term if index == 2 else both + term
        out = img_out[index - 2]
        out[...] = image_term((near, weights), texts, span).astype(out.dtype)
    if behind:
        total_out[...] = total
        both_out[...] = both
        return
    height = total.shape[0] // 2
    for index in range(2):
        part = total[index * height : (index + 1) * height]
        same_out[index][...] = part[:, :shard]
        cross_out[index][...] = part[:, shard:].astype(jnp.bfloat16)


def home_kernel(shard, span, *refs):
    below, (row_in, col_in, stat_ref) = refs[0:4], refs[4:7]
    images = (refs[7:8], refs[8:9])
    texts, (weights_in, both_in, *outs) = text_parts(refs[9:], 4)
    img_out, txt_own, txt_x = outs[0:2], *outs[2:]
    home = slice(0, 2 * shard)
    col_home = rows4(stat_ref, 4, home)
    total = both_in[...]
    for index in range(2):
        here = pl.ds(index * shard, shard)
        row = row_factors(stat_ref, (rows4(row_in, 0, here),), index, shard)
        tops = rows4(col_in, 4 * index, home)
        weights = weigh(below, here, home, row, tops, col_home)
        total = total + text_term(rows_of(images[index], span), weights)
        out = img_out[index]
        out[...] = image_term((weights, weights_in[here]), texts, span).astype(out.dtype)
    txt_own[...] = total[:, :shard]
    txt_x[...] = total[:, shard:].astype(jnp.bfloat16)


def add_kernel(first, second, out):
    total = first[...] + second[...].astype(jnp.float32)
    out[...] = total.astype(out.dtype)


def finish_image_kernel(scale, own, core, home, out):
    total = own[...] + core[...].astype(jnp.float32)
    out[...] = (total + home[...].astype(jnp.float32)) * scale


def finish_text_kernel(scale, own, x, *refs):
    homes, out = refs[:-1], refs[-1]
    width = homes[0].shape[0]
    for index, home in enumerate(homes):
        here = slice(index * width, (index + 1) * width)
        total = own[here] + x[here].astype(jnp.float32) + home[...].astype(jnp.float32)
        out[:, here] = total.T * scale


def on_device(student_image, student_text, teacher_image, teacher_text):
    shard, width_s = student_image.shape
    width_t = teacher_image.shape[1]
    scale_s = 2.0 / math.sqrt(width_s)
    scale_t = 2.0 / math.sqrt(width_t)
    f32 = jnp.float32
    bf16 = jnp.bfloat16
    vmem = pl.BlockSpec(memory_space=pltpu.VMEM)

    def params(mib):
        return pltpu.CompilerParams(vmem_limit_bytes=mib * MIB)


    spans = (slice(0, width_s), slice(width_s, width_s + width_t))
    scales = (scale_s, scale_t)

    def pack(first, second, *heights, name):
        heights = (shard, *heights)
        return pl.pallas_call(
            pack_kernel,
            out_shape=tuple(
                jax.ShapeDtypeStruct((height, width_s + width_t), bf16) for height in heights
            ),
            in_specs=[vmem] * 2,
            out_specs=(vmem,) * len(heights),
            compiler_params=params(8),
            name=name,
        )(first, second)

    text_t_ahead, text_t_x = ahead(teacher_text, -2), to_other_x(teacher_text)
    image_s_core, image_t_core = to_other_core(student_image), to_other_core(teacher_image)
    image, top, bottom = pack(
        student_image, teacher_image, shard * 9 // 16, shard * 7 // 16, name="pack_images"
    )
    bottom = send_to(bottom, lambda block, x, core: (block ^ 1, x, core))
    late_s, image_s_core, image_t_core = lax.optimization_barrier(
        (student_text, image_s_core, image_t_core)
    )
    text_s_ahead, text_s_x = ahead(late_s, -2), to_other_x(late_s)
    top, bottom, late_s, late_t = lax.optimization_barrier(
        (top, bottom, text_s_ahead, text_t_ahead, text_s_x, text_t_x)
    )[:4]
    packed, first = width_s + width_t, shard // 8
    text_ahead, rest, text_x, text_part = pl.pallas_call(
        pack_arrived_kernel,
        out_shape=tuple(
            jax.ShapeDtypeStruct((height, packed), bf16)
            for height in (shard, shard - first, shard, first)
        ),
        in_specs=[vmem] * 4,
        out_specs=(vmem,) * 4,
        compiler_params=params(8),
        name="pack_arrived",
    )(late_s, late_t, text_s_x, text_t_x)
    (text,) = pack(student_text, teacher_text, name="pack_own")
    (image_core,) = pack(image_s_core, image_t_core, name="pack_core")

    def stat(shards):
        return jax.ShapeDtypeStruct((8, shards * shard), f32)

    def score(rows, columns):
        return jax.ShapeDtypeStruct((rows * shard, columns * shard), f32)

    def part_scores(shards, texts, name, cost=None):
        sizes, count = tuple(len(parts) for parts in shards), {3: 3, 2: 1, 5: 4}[len(texts)]
        outs = (score(len(sizes), count),) * 4
        outs += (stat(len(sizes)), jax.ShapeDtypeStruct((4 * len(sizes), count * shard), f32))
        args = [part for parts in shards for part in parts] + list(texts)
        *below, row, col = pl.pallas_call(
            lambda *refs: part_kernel(shard, scales, spans, sizes, count, *refs),
            out_shape=outs,
            in_specs=[vmem] * len(args),
            out_specs=(vmem,) * len(outs),
            compiler_params=params(16),
            cost_estimate=cost,
            name=name,
        )(*args)
        return below, [row, col]

    text_both = (ahead(text_part, -2), to_other_x(rest))
    top = ahead(top, 1)
    bottom = send_to(bottom, lambda block, x, core: (block + 2 - block % 2 * 2, x, core))
    texts = (text, text_x, text_ahead, *text_both)
    own = ((image,), (image_core,))
    home, home_stats = part_scores(own, texts[:3], "scores_home")
    top, bottom = lax.optimization_barrier((top, bottom, home_stats[0]))[:2]
    behind = ((top, bottom), (to_other_core(top), to_other_core(bottom)))
    near, near_stats = part_scores(behind[:1], texts[:3], "scores_near")
    side, side_stats = part_scores((*own, behind[0]), texts[3:], "scores_side", HEAVY)
    others = (*home_stats, *near_stats, *side_stats)
    *far, far_row, far_col, partial = pl.pallas_call(
        lambda *refs: far_kernel(shard, scales, spans, *refs),
        out_shape=(score(1, 4),) * 4
        + (stat(1), jax.ShapeDtypeStruct((4, 4 * shard), f32), stat(4)),
        in_specs=[vmem] * 13,
        out_specs=(vmem,) * 7,
        compiler_params=params(16),
        name="scores_far",
    )(*behind[1], *texts, *others)
    images = (image, image_core, *behind[0], *behind[1])
    calls_stats = (*others, far_row, far_col)

    shared = jax.ShapeDtypeStruct((8, 2 * shard), f32)
    group, *away = pl.pallas_call(
        lambda *refs: join_group_kernel(shard, *refs),
        out_shape=(stat(4),) + (shared,) * 4,
        in_specs=[vmem] * 3,
        out_specs=(vmem,) * 5,
        compiler_params=params(8),
        name="join_group",
    )(partial, to_other_core(partial), to_other_x(partial))
    away = [
        send_to(away[index], lambda block, x, core, step=step, first=first: (
            block + (step if (block // step) % 2 == first else -step), x, core
        ))
        for index, step, first in ((0, 1, 0), (2, 2, 0), (1, 1, 1), (3, 2, 1))
    ]
    stats = pl.pallas_call(
        lambda *refs: join_blocks_kernel(shard, *refs),
        out_shape=stat(4),
        in_specs=[vmem] * 5,
        out_specs=vmem,
        compiler_params=params(8),
        name="join_blocks",
    )(group, *away)

    wide = jax.ShapeDtypeStruct((shard, width_s), f32)
    tall = jax.ShapeDtypeStruct((width_s, shard), f32)
    sent = jax.ShapeDtypeStruct((width_s, shard), bf16)
    flat = jax.ShapeDtypeStruct((shard, width_s), bf16)
    tall_half = jax.ShapeDtypeStruct((width_s // 2, shard), f32)
    sent_half = jax.ShapeDtypeStruct((width_s // 2, shard), bf16)
    square = jax.ShapeDtypeStruct((width_s, 2 * shard), f32)

    def gradients(behind, outs, *more, name):
        args = (
            *home, *near, *side, *far, *calls_stats, stats, *images, *texts, *more
        )
        return pl.pallas_call(
            lambda *refs: ahead_kernel(shard, spans[0], behind, *refs),
            out_shape=outs,
            in_specs=[vmem] * len(args),
            out_specs=(vmem,) * len(outs),
            compiler_params=params(24),
            name=name,
        )(*args)

    txt_part, img_back, img_cross, txt_both = gradients(
        True, (square, wide, flat, square), name="gradients_behind"
    )
    *txt_ahead, weights = gradients(
        False,
        (tall_half, tall_half, sent_half, sent_half)
        + (jax.ShapeDtypeStruct((2 * shard, 2 * shard), bf16),),
        txt_part,
        name="gradients_ahead",
    )
    img_cross = to_other_core(img_cross)
    img_sum = (img_back + img_cross.astype(f32)).astype(bf16)
    img_home = ahead(img_sum, -1)
    weights = lax.optimization_barrier((weights, img_sum))[0]
    img_own, img_core, txt_own, txt_x = pl.pallas_call(
        lambda *refs: home_kernel(shard, spans[0], *refs),
        out_shape=(wide, flat, tall, sent),
        in_specs=[vmem] * 16,
        out_specs=(vmem,) * 4,
        compiler_params=params(24),
        name="gradients_home",
    )(*home, *home_stats, stats, *images[:2], *texts, weights, txt_both)

    txt_same, txt_cross = txt_ahead[:2], [to_other_x(part) for part in txt_ahead[2:]]
    img_core = to_other_core(img_core)

    def add(first, second, out, name):
        return pl.pallas_call(
            add_kernel,
            out_shape=out,
            in_specs=[vmem] * 2,
            out_specs=vmem,
            compiler_params=params(8),
            cost_estimate=LIGHT,
            name=name,
        )(first, second)

    txt_cross[0] = lax.optimization_barrier((txt_cross[0], img_sum))[0]
    txt_sum = add(txt_same[0], txt_cross[0], sent_half, "add_text")
    txt_x, txt_cross[1] = lax.optimization_barrier((txt_x, txt_cross[1], txt_sum))[:2]
    txt_home = [
        ahead(txt_sum, 2), ahead(add(txt_same[1], txt_cross[1], sent_half, "add_text"), 2)
    ]
    txt_x = to_other_x(txt_x)

    def finish(kernel, *args, name, cost=None):
        return pl.pallas_call(
            lambda *refs: kernel(scale_s, *refs),
            out_shape=wide,
            in_specs=[vmem] * len(args),
            out_specs=vmem,
            compiler_params=params(8),
            cost_estimate=cost,
            name=name,
        )(*args)

    img_home, txt_x = lax.optimization_barrier((img_home, txt_x))
    grad_image = finish(
        finish_image_kernel, img_own, img_core, img_home, name="finish_image", cost=LIGHT
    )
    *txt_home, grad_image = lax.optimization_barrier((*txt_home, grad_image))
    grad_text = finish(finish_text_kernel, txt_own, txt_x, *txt_home, name="finish_text")
    return (grad_image, grad_text)


def solution(mesh):
    spec = P(AXES, None)
    return jax.shard_map(
        on_device,
        mesh=mesh,
        in_specs=(spec, spec, spec, spec),
        out_specs=(spec, spec),
        check_vma=False,
    )
```

```python
import math

import jax
import jax.numpy as jnp
from jax import lax
from jax.experimental import pallas as pl
from jax.experimental.pallas import tpu as pltpu
from jax.sharding import PartitionSpec as P

AXES = ("dp", "pair")
MIB = 1024 * 1024
LOG2E = math.log2(math.e)
HEAVY = pl.CostEstimate(flops=10**11, bytes_accessed=10**9, transcendentals=0)
LIGHT = pl.CostEstimate(flops=3 * 10**9, bytes_accessed=3 * 10**7, transcendentals=0)


def send_to(value, place):
    count = lax.axis_size("dp")
    pairs = []
    for block in range(count):
        for member in range(4):
            to_block, to_x, to_core = place(block, member // 2, member % 2)
            pairs.append((block * 4 + member, (to_block % count) * 4 + to_x * 2 + to_core))
    return lax.ppermute(value, AXES, pairs)


def to_other_core(value):
    return send_to(value, lambda block, x, core: (block, x, 1 - core))


def to_other_x(value):
    return send_to(value, lambda block, x, core: (block, 1 - x, core))


def ahead(value, steps):
    return send_to(value, lambda block, x, core: (block + steps, x, core))


def joined(first, second):
    rows = []
    for offset in (0, 2):
        rows += merged(first[offset : offset + 2], second[offset : offset + 2])
    return rows


def pack_kernel(first, second, whole, *parts):
    width = first.shape[1]
    whole[:, :width] = first[...]
    whole[:, width:] = second[...]
    start = 0
    for out in parts:
        here = pl.ds(start, out.shape[0])
        out[:, :width] = first[here]
        out[:, width:] = second[here]
        start += out.shape[0]


def pack_arrived_kernel(s_ahead, t_ahead, s_x, t_x, ahead_out, rest_out, x_out, part_out):
    width, first = s_x.shape[1], part_out.shape[0]
    for student, teacher, whole, part, here in (
        (s_ahead, t_ahead, ahead_out, rest_out, pl.ds(first, s_x.shape[0] - first)),
        (s_x, t_x, x_out, part_out, pl.ds(0, first)),
    ):
        whole[:, :width] = student[...]
        whole[:, width:] = teacher[...]
        part[:, :width] = student[here]
        part[:, width:] = teacher[here]


def rows_of(parts, columns):
    parts = [part[:, columns] for part in parts]
    return parts[0] if len(parts) == 1 else jnp.concatenate(parts, axis=0)


def tile_of(image, texts, span, scale):
    parts = [
        lax.dot_general(
            image,
            rows_of(text, span),
            (((1,), (1,)), ((), ())),
            preferred_element_type=jnp.float32,
        )
        for text in texts
    ]
    tile = parts[0] if len(parts) == 1 else jnp.concatenate(parts, axis=1)
    return tile * (scale * LOG2E)


def stats_along(tile, axis):
    top = jnp.max(tile, axis=axis, keepdims=True)
    below = jnp.exp2(tile - top)
    return top, jnp.sum(below, axis=axis, keepdims=True), below


def merged(first, second):
    top = jnp.maximum(first[0], second[0])
    return top, first[1] * jnp.exp2(first[0] - top) + second[1] * jnp.exp2(second[0] - top)


def as_rows(columns, shard):
    lane = lax.broadcasted_iota(jnp.int32, (shard, 128), 1)
    packed = jnp.zeros((shard, 128), jnp.float32)
    for k, column in enumerate(columns):
        packed = jnp.where(lane == k, column, packed)
    return packed.T[:8]


def score_shards(images, texts, spans, scales, outs, shard):
    stats = [([], []) for _ in images]
    waiting = None
    for step in [(index, which) for index in range(len(images)) for which in range(2)] + [None]:
        tile = None
        if step:
            index, which = step
            image = rows_of(images[index], spans[which])
            tile = tile_of(image, texts, spans[which], scales[which])
        if waiting:
            (index, which), old = waiting
            here = pl.ds(index * shard, shard)
            for axis, found in ((1, stats[index][0]), (0, stats[index][1])):
                top, total, outs[2 * which + 1 - axis][here] = stats_along(old, axis)
                found += (top, total)
        waiting = step, tile
    return stats


def rows4(ref, first, columns=slice(None)):
    part = ref[first : first + 4, columns]
    return [part[k : k + 1] for k in range(4)]


def text_parts(refs, count):
    whole = count - 1
    texts = [(ref,) for ref in refs[:whole]]
    if count == 3:
        return texts + [refs[whole : whole + 1]], refs[whole + 1 :]
    return texts + [refs[whole : whole + 2]], refs[whole + 2 :]


def part_kernel(shard, scales, spans, sizes, count, *refs):
    images = []
    for size in sizes:
        images.append(refs[:size])
        refs = refs[size:]
    texts, refs = text_parts(refs, count)
    outs, (row_out, col_out) = refs[:4], refs[4:]
    stats = score_shards(images, texts, spans, scales, outs, shard)
    for index, (row, column) in enumerate(stats):
        row_out[:, pl.ds(index * shard, shard)] = as_rows(row, shard)
        for k, value in enumerate(column):
            col_out[4 * index + k : 4 * index + k + 1] = value


def far_kernel(shard, scales, spans, *refs):
    outs = refs[13:]
    part_kernel(shard, scales, spans, (2,), 4, *refs[:7], *outs[:6])
    total_kernel(shard, *refs[7:13], *outs[4:])


HOME, NEAR, SIDE, FAR = range(4)


def join_calls(rows_in, cols_in, shard):
    rows = []
    for index in range(3):
        call, place = (HOME, index) if index < 2 else (NEAR, 0)
        first = rows4(rows_in[call], 0, pl.ds(place * shard, shard))
        rows.append(joined(first, rows4(rows_in[SIDE], 0, pl.ds(index * shard, shard))))
    rows.append(rows4(rows_in[FAR], 0))
    columns = rows4(cols_in[FAR], 0)
    seen = [part[:, : 3 * shard] for part in columns]
    last = [part[:, 3 * shard :] for part in columns]
    for call, place in ((HOME, 0), (HOME, 1), (NEAR, 0)):
        seen = joined(seen, rows4(cols_in[call], 4 * place))
    for place in range(3):
        last = joined(last, rows4(cols_in[SIDE], 4 * place))
    return rows, seen, last


def total_kernel(shard, *refs):
    rows, seen, last = join_calls(refs[0:8:2], refs[1:8:2], shard)
    row_out, col_out = refs[8:]
    for k in range(4):
        for index in range(4):
            row_out[k : k + 1, index * shard : (index + 1) * shard] = rows[index][k]
        col_out[k : k + 1, : 3 * shard] = seen[k]
        col_out[k : k + 1, 3 * shard :] = last[k]


def piece_stats(ref, kind, piece, shard):
    part = ref[4 * kind : 4 * kind + 4, piece * shard : (piece + 1) * shard]
    return [part[k : k + 1] for k in range(4)]


def block_parities():
    block = lax.axis_index("dp")
    return lax.rem(block, 2) == 0, lax.rem(block // 2, 2) == 0


def join_group_kernel(shard, row_ref, col_ref, core_ref, x_ref, home_ref, *outs):
    halves = []
    for kind, (mine_ref, other_ref) in enumerate(((row_ref, core_ref), (col_ref, x_ref))):
        for half in range(2):
            joint = []
            for piece in (2 * half, 2 * half + 1):
                total = joined(
                    piece_stats(mine_ref, 0, piece, shard),
                    piece_stats(other_ref, 0, piece ^ 1, shard),
                )
                for k, value in enumerate(total):
                    at = 4 * kind + k
                    home_ref[at : at + 1, piece * shard : (piece + 1) * shard] = value
                joint.append(total)
            halves.append([jnp.concatenate(pair, axis=1) for pair in zip(*joint)])
    for kind, upward in enumerate(block_parities()):
        up, down = halves[2 * kind + kind], halves[2 * kind + 1 - kind]
        for k in range(4):
            outs[2 * kind][k : k + 1] = jnp.where(upward, up[k], down[k])
            outs[2 * kind + 1][k : k + 1] = jnp.where(upward, down[k], up[k])


def join_blocks_kernel(shard, home_ref, *refs):
    ins, out = refs[:4], refs[4]
    for kind, upward in enumerate(block_parities()):
        first, second = (rows4(ref, 0) for ref in ins[kind::2])
        above = [jnp.where(upward, x, y) for x, y in zip(first, second)]
        below = [jnp.where(upward, y, x) for x, y in zip(first, second)]
        for half in range(2):
            here = slice(2 * half * shard, 2 * (half + 1) * shard)
            total = joined(rows4(home_ref, 4 * kind, here), above if half == kind else below)
            for k, value in enumerate(total):
                at = 4 * kind + k
                out[at : at + 1, here] = value


def row_factors(stat_ref, tops, index, shard):
    max_s, total_s, max_t, total_t = rows4(stat_ref, 0, pl.ds(index * shard, shard))
    sub = lax.broadcasted_iota(jnp.int32, (128, shard), 0)
    packed = jnp.zeros((128, shard), jnp.float32)
    for k, (top_s, _, top_t, _) in enumerate(tops):
        packed = jnp.where(sub == 2 * k, jnp.exp2(top_s - max_s) / total_s, packed)
        packed = jnp.where(sub == 2 * k + 1, jnp.exp2(top_t - max_t) / total_t, packed)
    packed = packed.T
    return [packed[:, k : k + 1] for k in range(2 * len(tops))]


def weigh(below, here, columns, row, tops, stats):
    row_s, col_s, row_t, col_t = (ref[here, columns] for ref in below)
    top_s, _, top_t, _ = tops
    max_s, total_s, max_t, total_t = stats
    return (
        row_s * row[0]
        - row_t * row[1]
        + col_s * (jnp.exp2(top_s - max_s) / total_s)
        - col_t * (jnp.exp2(top_t - max_t) / total_t)
    ).astype(jnp.bfloat16)


def text_term(image, weights):
    return lax.dot_general(
        image, weights, (((0,), (0,)), ((), ())), preferred_element_type=jnp.float32
    )


def image_term(weights, texts, span):
    total = None
    for index, text in enumerate(texts):
        shard = weights[0].shape[1] // 2
        part = jnp.dot(
            weights[index // 2][:, (index % 2) * shard : (index % 2 + 1) * shard],
            rows_of(text, span),
            preferred_element_type=jnp.float32,
        )
        total = part if total is None else total + part
    return total


def ahead_kernel(shard, span, *refs):
    below, refs = (refs[0:4], refs[4:8], refs[8:12], refs[12:16]), refs[16:]
    rows_in, cols_in, stat_ref = refs[0:8:2], refs[1:8:2], refs[8]
    images = (refs[9:10], refs[10:11], refs[11:13], refs[13:15])
    texts, refs = text_parts(refs[15:], 4)
    same_out, cross_out, weights_out, img_out, both_out = (
        refs[0:2], refs[2:4], refs[4], refs[5:7], refs[7]
    )
    home, third = slice(0, 2 * shard), slice(2 * shard, 3 * shard)
    fourth, far = slice(3 * shard, 4 * shard), slice(2 * shard, 4 * shard)
    col_home, col_third, col_last, col_far = (
        rows4(stat_ref, 4, at) for at in (home, third, fourth, far)
    )

    def weights_of(index):
        if index == 3:
            here = pl.ds(0, shard)
            row = row_factors(stat_ref, (rows4(rows_in[FAR], 0),), index, shard)
            weights, near = (
                weigh(below[FAR], here, at, row, rows4(cols_in[FAR], 0, at), columns)
                for at, columns in ((far, col_far), (home, col_home))
            )
            return weights, near
        call, place = (HOME, index) if index < 2 else (NEAR, 0)
        here, side = pl.ds(place * shard, shard), pl.ds(index * shard, shard)
        tops = (rows4(rows_in[call], 0, here), rows4(rows_in[SIDE], 0, side))
        row = row_factors(stat_ref, tops, index, shard)
        seen = rows4(cols_in[call], 4 * place, third)
        weights = [weigh(below[call], here, third, row[:2], seen, col_third)]
        seen = rows4(cols_in[SIDE], 4 * index)
        weights.append(weigh(below[SIDE], side, slice(None), row[2:], seen, col_last))
        near = None
        if index == 2:
            seen = rows4(cols_in[call], 4 * place, home)
            near = weigh(below[call], here, home, row[:2], seen, col_home)
        return jnp.concatenate(weights, axis=1), near

    total = both = None
    ready = weights_of(0)
    for index in range(4):
        weights, near = ready
        if index < 3:
            ready = weights_of(index + 1)
        image = rows_of(images[index], span)
        term = text_term(image, weights)
        total = total + term if index else term
        if index < 2:
            weights_out[pl.ds(index * shard, shard)] = weights
            continue
        term = text_term(image, near)
        both = term if index == 2 else both + term
        out = img_out[index - 2]
        out[...] = image_term((near, weights), texts, span).astype(out.dtype)
    height = total.shape[0] // 2
    for index in range(2):
        part = total[index * height : (index + 1) * height]
        same_out[index][...] = part[:, :shard]
        cross_out[index][...] = part[:, shard:].astype(jnp.bfloat16)
    both_out[...] = both


def home_kernel(shard, span, *refs):
    below, (row_in, col_in, stat_ref) = refs[0:4], refs[4:7]
    images = (refs[7:8], refs[8:9])
    texts, (weights_in, both_in, *outs) = text_parts(refs[9:], 4)
    img_out, txt_own, txt_x = outs[0:2], *outs[2:]
    home = slice(0, 2 * shard)
    col_home = rows4(stat_ref, 4, home)
    total = both_in[...]
    for index in range(2):
        here = pl.ds(index * shard, shard)
        row = row_factors(stat_ref, (rows4(row_in, 0, here),), index, shard)
        tops = rows4(col_in, 4 * index, home)
        weights = weigh(below, here, home, row, tops, col_home)
        total = total + text_term(rows_of(images[index], span), weights)
        out = img_out[index]
        out[...] = image_term((weights, weights_in[here]), texts, span).astype(out.dtype)
    txt_own[...] = total[:, :shard]
    txt_x[...] = total[:, shard:].astype(jnp.bfloat16)


def add_kernel(first, second, out):
    total = first[...] + second[...].astype(jnp.float32)
    out[...] = total.astype(out.dtype)


def finish_image_kernel(scale, own, core, home, out):
    total = own[...] + core[...].astype(jnp.float32)
    out[...] = (total + home[...].astype(jnp.float32)) * scale


def finish_text_kernel(scale, own, x, *refs):
    homes, out = refs[:-1], refs[-1]
    width = homes[0].shape[0]
    for index, home in enumerate(homes):
        here = slice(index * width, (index + 1) * width)
        total = own[here] + x[here].astype(jnp.float32) + home[...].astype(jnp.float32)
        out[:, here] = total.T * scale


def on_device(student_image, student_text, teacher_image, teacher_text):
    shard, width_s = student_image.shape
    width_t = teacher_image.shape[1]
    scale_s = 2.0 / math.sqrt(width_s)
    scale_t = 2.0 / math.sqrt(width_t)
    f32 = jnp.float32
    bf16 = jnp.bfloat16
    vmem = pl.BlockSpec(memory_space=pltpu.VMEM)

    def params(mib):
        return pltpu.CompilerParams(vmem_limit_bytes=mib * MIB)


    spans = (slice(0, width_s), slice(width_s, width_s + width_t))
    scales = (scale_s, scale_t)

    def pack(first, second, *heights, name):
        heights = (shard, *heights)
        return pl.pallas_call(
            pack_kernel,
            out_shape=tuple(
                jax.ShapeDtypeStruct((height, width_s + width_t), bf16) for height in heights
            ),
            in_specs=[vmem] * 2,
            out_specs=(vmem,) * len(heights),
            compiler_params=params(8),
            name=name,
        )(first, second)

    text_t_ahead, text_t_x = ahead(teacher_text, -2), to_other_x(teacher_text)
    image_s_core, image_t_core = to_other_core(student_image), to_other_core(teacher_image)
    image, top, bottom = pack(
        student_image, teacher_image, shard * 9 // 16, shard * 7 // 16, name="pack_images"
    )
    bottom = send_to(bottom, lambda block, x, core: (block ^ 1, x, core))
    late_s, image_s_core, image_t_core = lax.optimization_barrier(
        (student_text, image_s_core, image_t_core)
    )
    text_s_ahead, text_s_x = ahead(late_s, -2), to_other_x(late_s)
    top, bottom, late_s, late_t = lax.optimization_barrier(
        (top, bottom, text_s_ahead, text_t_ahead, text_s_x, text_t_x)
    )[:4]
    packed, first = width_s + width_t, shard // 8
    text_ahead, rest, text_x, text_part = pl.pallas_call(
        pack_arrived_kernel,
        out_shape=tuple(
            jax.ShapeDtypeStruct((height, packed), bf16)
            for height in (shard, shard - first, shard, first)
        ),
        in_specs=[vmem] * 4,
        out_specs=(vmem,) * 4,
        compiler_params=params(8),
        name="pack_arrived",
    )(late_s, late_t, text_s_x, text_t_x)
    (text,) = pack(student_text, teacher_text, name="pack_own")
    (image_core,) = pack(image_s_core, image_t_core, name="pack_core")

    def stat(shards):
        return jax.ShapeDtypeStruct((8, shards * shard), f32)

    def score(rows, columns):
        return jax.ShapeDtypeStruct((rows * shard, columns * shard), f32)

    def part_scores(shards, texts, name, cost=None):
        sizes, count = tuple(len(parts) for parts in shards), {3: 3, 2: 1, 5: 4}[len(texts)]
        outs = (score(len(sizes), count),) * 4
        outs += (stat(len(sizes)), jax.ShapeDtypeStruct((4 * len(sizes), count * shard), f32))
        args = [part for parts in shards for part in parts] + list(texts)
        *below, row, col = pl.pallas_call(
            lambda *refs: part_kernel(shard, scales, spans, sizes, count, *refs),
            out_shape=outs,
            in_specs=[vmem] * len(args),
            out_specs=(vmem,) * len(outs),
            compiler_params=params(16),
            cost_estimate=cost,
            name=name,
        )(*args)
        return below, [row, col]

    text_both = (ahead(text_part, -2), to_other_x(rest))
    top = ahead(top, 1)
    bottom = send_to(bottom, lambda block, x, core: (block + 2 - block % 2 * 2, x, core))
    texts = (text, text_x, text_ahead, *text_both)
    own = ((image,), (image_core,))
    home, home_stats = part_scores(own, texts[:3], "scores_home")
    top, bottom = lax.optimization_barrier((top, bottom, home_stats[0]))[:2]
    behind = ((top, bottom), (to_other_core(top), to_other_core(bottom)))
    near, near_stats = part_scores(behind[:1], texts[:3], "scores_near")
    side, side_stats = part_scores((*own, behind[0]), texts[3:], "scores_side", HEAVY)
    others = (*home_stats, *near_stats, *side_stats)
    *far, far_row, far_col, partial_row, partial_col = pl.pallas_call(
        lambda *refs: far_kernel(shard, scales, spans, *refs),
        out_shape=(score(1, 4),) * 4
        + (stat(1),) + (jax.ShapeDtypeStruct((4, 4 * shard), f32),) * 3,
        in_specs=[vmem] * 13,
        out_specs=(vmem,) * 8,
        compiler_params=params(16),
        name="scores_far",
    )(*behind[1], *texts, *others)
    images = (image, image_core, *behind[0], *behind[1])
    calls_stats = (*others, far_row, far_col)

    shared = jax.ShapeDtypeStruct((4, 2 * shard), f32)
    group, *away = pl.pallas_call(
        lambda *refs: join_group_kernel(shard, *refs),
        out_shape=(stat(4),) + (shared,) * 4,
        in_specs=[vmem] * 4,
        out_specs=(vmem,) * 5,
        compiler_params=params(8),
        name="join_group",
    )(partial_row, partial_col, to_other_core(partial_row), to_other_x(partial_col))
    away = [
        send_to(away[index], lambda block, x, core, step=step, first=first: (
            block + (step if (block // step) % 2 == first else -step), x, core
        ))
        for index, step, first in ((0, 1, 0), (2, 2, 0), (1, 1, 1), (3, 2, 1))
    ]
    stats = pl.pallas_call(
        lambda *refs: join_blocks_kernel(shard, *refs),
        out_shape=stat(4),
        in_specs=[vmem] * 5,
        out_specs=vmem,
        compiler_params=params(8),
        name="join_blocks",
    )(group, *away)

    wide = jax.ShapeDtypeStruct((shard, width_s), f32)
    tall = jax.ShapeDtypeStruct((width_s, shard), f32)
    sent = jax.ShapeDtypeStruct((width_s, shard), bf16)
    flat = jax.ShapeDtypeStruct((shard, width_s), bf16)
    tall_half = jax.ShapeDtypeStruct((width_s // 2, shard), f32)
    sent_half = jax.ShapeDtypeStruct((width_s // 2, shard), bf16)
    *txt_ahead, weights, img_back, img_cross, txt_both = pl.pallas_call(
        lambda *refs: ahead_kernel(shard, spans[0], *refs),
        out_shape=(
            tall_half,
            tall_half,
            sent_half,
            sent_half,
            jax.ShapeDtypeStruct((2 * shard, 2 * shard), bf16),
            wide,
            flat,
            jax.ShapeDtypeStruct((width_s, 2 * shard), f32),
        ),
        in_specs=[vmem] * 36,
        out_specs=(vmem,) * 8,
        compiler_params=params(24),
        name="gradients_ahead",
    )(
        *home, *near, *side, *far, *calls_stats, stats,
        *images, *texts,
    )
    img_cross = to_other_core(img_cross)
    img_sum = (img_back + img_cross.astype(f32)).astype(bf16)
    img_home = ahead(img_sum, -1)
    weights = lax.optimization_barrier((weights, img_sum))[0]
    img_own, img_core, txt_own, txt_x = pl.pallas_call(
        lambda *refs: home_kernel(shard, spans[0], *refs),
        out_shape=(wide, flat, tall, sent),
        in_specs=[vmem] * 16,
        out_specs=(vmem,) * 4,
        compiler_params=params(24),
        name="gradients_home",
    )(*home, *home_stats, stats, *images[:2], *texts, weights, txt_both)

    txt_same, txt_cross = txt_ahead[:2], [to_other_x(part) for part in txt_ahead[2:]]
    img_core = to_other_core(img_core)

    def add(first, second, out, name):
        return pl.pallas_call(
            add_kernel,
            out_shape=out,
            in_specs=[vmem] * 2,
            out_specs=vmem,
            compiler_params=params(8),
            cost_estimate=LIGHT,
            name=name,
        )(first, second)

    txt_cross[0] = lax.optimization_barrier((txt_cross[0], img_sum))[0]
    txt_sum = add(txt_same[0], txt_cross[0], sent_half, "add_text")
    txt_x, txt_cross[1] = lax.optimization_barrier((txt_x, txt_cross[1], txt_sum))[:2]
    txt_home = [
        ahead(txt_sum, 2), ahead(add(txt_same[1], txt_cross[1], sent_half, "add_text"), 2)
    ]
    txt_x = to_other_x(txt_x)

    def finish(kernel, *args, name, cost=None):
        return pl.pallas_call(
            lambda *refs: kernel(scale_s, *refs),
            out_shape=wide,
            in_specs=[vmem] * len(args),
            out_specs=vmem,
            compiler_params=params(8),
            cost_estimate=cost,
            name=name,
        )(*args)

    img_home, txt_x = lax.optimization_barrier((img_home, txt_x))
    grad_image = finish(
        finish_image_kernel, img_own, img_core, img_home, name="finish_image", cost=LIGHT
    )
    *txt_home, grad_image = lax.optimization_barrier((*txt_home, grad_image))
    grad_text = finish(finish_text_kernel, txt_own, txt_x, *txt_home, name="finish_text")
    return (grad_image, grad_text)


def solution(mesh):
    spec = P(AXES, None)
    return jax.shard_map(
        on_device,
        mesh=mesh,
        in_specs=(spec, spec, spec, spec),
        out_specs=(spec, spec),
        check_vma=False,
    )
```
